256 devices in a mesh: tiles: 256 (over z, x, y, core).
Axes of the slice: x: 4, y: 4, z: 8, core: 2. Of those that a mesh axis runs over, the one named last changes fastest.
Arguments:
- ocean_state: bfloat16 [1024, 32, 32, 95], P('tiles'), may hold values from -6 to 6
- cotangent: bfloat16 [1024, 32, 32, 192], P('tiles'), may hold values from -6 to 6
- w_stem: bfloat16 [95, 192], replicated, may hold values from -0.625 to 0.625
- dw_kernel: bfloat16 [7, 7, 192], replicated, may hold values from -0.875 to 0.875
- norm_gain: float32 [192], replicated, may hold values from 0.25 to 1.75
- w_up: bfloat16 [192, 768], replicated, may hold values from -0.4375 to 0.4375
- w_down: bfloat16 [768, 192], replicated, may hold values from -0.21875 to 0.21875
- tile_links: int32 [1024, 4], P('tiles'), may hold values from -1 to 3, as said below
- fold_flags: int32 [1024], P('tiles'), may hold values from 0 to 1, as said below
- wet_count: int32 [256], P('tiles'), may hold values from 1 to 4, as said below
Outputs:
- grad_state: bfloat16 [1024, 32, 32, 95], P('tiles')
- grad_stem: float32 [95, 192], replicated
- grad_kernel: float32 [7, 7, 192], replicated
- grad_gain: float32 [192], replicated
- grad_up: float32 [192, 768], replicated
- grad_down: float32 [768, 192], replicated
The draws below stay inside these ranges and needn't reach their ends.
Inputs may be any that keep to these rules, and one draw needn't show every extreme that they name: `tile_links`: each slot's west and east links name a slot of the device before and after it (wrapping), its south and north links a slot of its own device, -1 for land, outside the grid and across the fold. Links are mutual: a slot's east neighbour has it as west neighbour, its north neighbour has it as south neighbour. Empty slots have -1 in every column and no link names them. `fold_flags`: at most one slot a device is marked, a live tile of the top tile row; device d's mark equals its mirror device's mark. Live slots are slots 0 to wet_count - 1 of a device; some device is full.
All inputs are finite; a program needn't handle non-finite values.
Results may differ from the reference program's by a relative error of at most 0.0071.
Values may be sent and summed in bfloat16 or wider, within the bound.
No kernel may reach another device: no remote copies, remote signals or barrier semaphores. Data moves between devices by JAX's collectives and lax.ppermute only.
A program may use at most 128 MiB of HBM per device.

```python
import jax
import jax.numpy as jnp
from jax import lax

CIN = 95
CH = 192
FFN = 768
TS = 32
TILE_ROWS = 4
TILES = 1024
N_TILES = 256


def tile_layout(key):
    columns = N_TILES
    row_count = TILE_ROWS
    rolled = jax.random.randint(key, (columns, row_count), 0, 100)
    column_ids = jnp.arange(columns, dtype=jnp.int32)[:, None]
    row_ids = jnp.arange(row_count, dtype=jnp.int32)[None, :]
    wet_tiles = (rolled < 50) | (column_ids == 0) | (row_ids == row_count // 2) | (column_ids == columns - 1) & (row_ids == row_count - 1)
    wet_ints = wet_tiles.astype(jnp.int32)
    filled = jnp.cumsum(wet_ints, axis=1, dtype=jnp.int32)
    wet_total = filled[:, -1]
    slot_ids = jnp.arange(row_count, dtype=jnp.int32)
    row_of = jnp.sum((filled[:, None, :] <= slot_ids[None, :, None]).astype(jnp.int32), axis=2, dtype=jnp.int32)
    active = slot_ids[None, :] < wet_total[:, None]
    row_safe = jnp.minimum(row_of, row_count - 1).astype(jnp.int32)

    def beside(shift_by):
        wet_near = jnp.roll(wet_ints, shift_by, axis=0)
        filled_near = jnp.roll(filled, shift_by, axis=0)
        present = jnp.take_along_axis(wet_near, row_safe, axis=1)
        target = jnp.take_along_axis(filled_near, row_safe, axis=1) - 1
        return jnp.where(active & (present == 1), target, -1)
    west_link = beside(1)
    east_link = beside(-1)
    row_below = row_safe - 1
    below_wet = jnp.take_along_axis(wet_ints, jnp.maximum(row_below, 0), axis=1)
    south_link = jnp.where(active & (row_below >= 0) & (below_wet == 1), slot_ids[None, :] - 1, -1)
    row_above = row_safe + 1
    above_wet = jnp.take_along_axis(wet_ints, jnp.minimum(row_above, row_count - 1), axis=1)
    north_link = jnp.where(active & (row_above < row_count) & (above_wet == 1), slot_ids[None, :] + 1, -1)
    mirror_top = jnp.roll(wet_ints, columns // 2, axis=0)[:, row_count - 1][:, None]
    flags = (active & (row_safe == row_count - 1) & (wet_ints[:, row_count - 1][:, None] == 1) & (mirror_top == 1)).astype(jnp.int32)
    links = jnp.stack([west_link, east_link, south_link, north_link], axis=-1).astype(jnp.int32)
    return (links.reshape(columns * row_count, 4), flags.reshape(columns * row_count), wet_total.astype(jnp.int32))


def draw_tile_links(key, part):
    layout = tile_layout(key)
    return layout[0]


def draw_fold_flags(key, part):
    layout = tile_layout(key)
    return layout[1]


def draw_wet_count(key, part):
    layout = tile_layout(key)
    return layout[2]


def steps_of(rng, extent, split, least, top_value):
    level, own = 1.0, jax.random.fold_in(rng, 6)
    for position, parts in split:
        heights = jnp.exp(jax.random.uniform(jax.random.fold_in(own, position), (parts,), jnp.float32, least / len(split), top_value / len(split)))
        level = level * jnp.repeat(heights, extent[position] // parts).reshape([-1 if axis == position else 1 for axis in range(len(extent))])
    return level


def normal_values(stream_key, dims, scale, bound, split=(), kind=jnp.bfloat16):
    factor_of = steps_of(stream_key, dims, split, -0.22, 0.18) if split else 1.0
    array = jax.random.normal(stream_key, dims, jnp.float32) * scale * factor_of
    return jnp.minimum(jnp.maximum(array, -bound), bound).astype(kind)


def setup_inputs(seed: int = 0) -> dict:
    keys = jax.random.split(jax.random.key(seed), 11)
    return {
        "ocean_state": normal_values(keys[0], (TILES, TS, TS, CIN), 1.0, 6.0, ((0, 256),)),
        "cotangent": normal_values(keys[1], (TILES, TS, TS, CH), 1.0, 6.0, ((0, 256),)),
        "w_stem": normal_values(keys[2], (CIN, CH), CIN ** -0.5, 0.625),
        "dw_kernel": normal_values(keys[3], (7, 7, CH), 49 ** -0.5, 0.875),
        "norm_gain": jnp.clip(1.0 + 0.15 * jax.random.normal(keys[4], (CH,), jnp.float32), 0.25, 1.75),
        "w_up": normal_values(keys[5], (CH, FFN), CH ** -0.5, 0.4375),
        "w_down": normal_values(keys[6], (FFN, CH), FFN ** -0.5, 0.21875),
        "tile_links": draw_tile_links(jax.random.fold_in(keys[10], 71), 0),
        "fold_flags": draw_fold_flags(jax.random.fold_in(keys[10], 71), 0),
        "wet_count": draw_wet_count(jax.random.fold_in(keys[10], 71), 0),
    }


epsilon = 1e-06
root_half = 0.7071067811865476
inv_root_two_pi = 0.3989422804014327

def gelu_exact(hidden):
    return 0.5 * hidden * (1.0 + lax.erf(hidden * root_half))

def gelu_slope(hidden):
    return 0.5 * (1.0 + lax.erf(hidden * root_half)) + hidden * jnp.exp(-0.5 * hidden * hidden) * inv_root_two_pi

def tile_step(extended, cot_tile, dw_kernel, norm_gain, w_up, w_down):
    tile_side = cot_tile.shape[0]
    model_width = cot_tile.shape[2]
    ext_full = extended.astype(jnp.float32)
    kernel_full = dw_kernel.astype(jnp.float32)
    mixed = jnp.zeros((tile_side, tile_side, model_width), jnp.float32)
    for row_off in range(7):
        for col_off in range(7):
            mixed = mixed + ext_full[row_off:row_off + tile_side, col_off:col_off + tile_side] * kernel_full[row_off, col_off]
    average = lax.optimization_barrier(jnp.mean(mixed, axis=-1, keepdims=True))
    centred = mixed - average
    variance = lax.optimization_barrier(jnp.mean(centred * centred, axis=-1, keepdims=True))
    inv_std = lax.rsqrt(variance + epsilon)
    normed = centred * inv_std
    normed_low = (normed * norm_gain).astype(jnp.bfloat16).reshape(-1, model_width)
    hidden = jnp.dot(normed_low, w_up, preferred_element_type=jnp.float32)
    activated = gelu_exact(hidden).astype(jnp.bfloat16)
    cot_flat = cot_tile.reshape(-1, model_width)
    grad_down = jnp.dot(activated.T, cot_flat, preferred_element_type=jnp.float32)
    grad_act = jnp.dot(cot_flat, w_down.T, preferred_element_type=jnp.float32)
    grad_hidden = (grad_act * gelu_slope(hidden)).astype(jnp.bfloat16)
    grad_up = jnp.dot(normed_low.T, grad_hidden, preferred_element_type=jnp.float32)
    grad_normed = jnp.dot(grad_hidden, w_up.T, preferred_element_type=jnp.float32).reshape(tile_side, tile_side, model_width)
    grad_gain = lax.optimization_barrier(jnp.sum(grad_normed * normed, axis=(0, 1)))
    grad_unit = grad_normed * norm_gain
    grad_mixed = inv_std * (grad_unit - lax.optimization_barrier(jnp.mean(grad_unit, axis=-1, keepdims=True)) - normed * lax.optimization_barrier(jnp.mean(grad_unit * normed, axis=-1, keepdims=True)))
    padded = jnp.pad(grad_mixed, ((6, 6), (6, 6), (0, 0)))
    grad_ext = jnp.zeros((tile_side + 6, tile_side + 6, model_width), jnp.float32)
    kernel_terms = []
    for row_off in range(7):
        for col_off in range(7):
            kernel_terms.append(lax.optimization_barrier(jnp.sum(ext_full[row_off:row_off + tile_side, col_off:col_off + tile_side] * grad_mixed, axis=(0, 1))))
            grad_ext = grad_ext + padded[6 - row_off:12 - row_off + tile_side, 6 - col_off:12 - col_off + tile_side] * kernel_full[row_off, col_off]
    grad_kernel = jnp.stack(kernel_terms).reshape(7, 7, model_width)
    return (grad_ext, grad_kernel, grad_gain, grad_up, grad_down)

def select_slots(source, link_col):
    safe_index = jnp.clip(link_col.astype(jnp.int32), 0, source.shape[0] - 1).astype(jnp.int32)
    picked = jnp.take(source, safe_index, axis=0)
    keep = (link_col >= 0).reshape((-1,) + (1,) * (source.ndim - 1))
    return jnp.where(keep, picked, jnp.zeros_like(picked))

def mirror(strips):
    return strips[::-1, ::-1]

def fold_rows(strips, flags):
    chosen = jnp.where((flags == 1)[:, None, None, None], strips.astype(jnp.float32), 0.0)
    return lax.optimization_barrier(jnp.sum(chosen, axis=0)).astype(jnp.bfloat16)

def widen(stem_mid, stem_west, stem_east, links):
    tile_side = stem_mid.shape[1]
    west_cols = select_slots(stem_west[:, :, tile_side - 3:], links[:, 0])
    east_cols = select_slots(stem_east[:, :, :3], links[:, 1])
    return jnp.concatenate([west_cols, stem_mid, east_cols], axis=2)

def extend(widened, links, flags, partner_rows):
    tile_side = widened.shape[1]
    south_rows = select_slots(widened[:, tile_side - 3:], links[:, 2])
    north_rows = select_slots(widened[:, :3], links[:, 3])
    north_rows = jnp.where((flags == 1)[:, None, None, None], mirror(partner_rows)[None], north_rows)
    return jnp.concatenate([south_rows, widened, north_rows], axis=1)

def reference(ocean_state, cotangent, w_stem, dw_kernel, norm_gain, w_up, w_down, tile_links, fold_flags, wet_count):
    devices = int(N_TILES)
    half_devices = devices // 2
    tile_side = int(TS)
    slot_total = int(TILE_ROWS)
    states = ocean_state.reshape(devices, slot_total, tile_side, tile_side, CIN)
    cotans = cotangent.reshape(devices, slot_total, tile_side, tile_side, CH)
    links_all = tile_links.reshape(devices, slot_total, 4)
    flags_all = fold_flags.reshape(devices, slot_total)
    slot_ids = jnp.arange(slot_total, dtype=jnp.int32)

    def stem_of(states_dev):
        product = jnp.dot(states_dev.reshape(-1, CIN), w_stem, preferred_element_type=jnp.float32)
        return product.astype(jnp.bfloat16).reshape(slot_total, tile_side, tile_side, CH)
    stem_all = lax.map(stem_of, states)

    def moved(device, offset):
        total = jnp.asarray(devices, dtype=jnp.int32)
        shifted = device.astype(jnp.int32) + jnp.asarray(offset + devices, dtype=jnp.int32)
        return lax.rem(shifted, total).astype(jnp.int32)

    def widened_at(device):
        return widen(stem_all[device], stem_all[moved(device, -1)], stem_all[moved(device, 1)], links_all[device])

    def masked_cot(device):
        active = slot_ids < wet_count[device].astype(jnp.int32)
        return jnp.where(active[:, None, None, None], cotans[device], jnp.zeros_like(cotans[device]))

    def first_pass(running, device):
        partner_dev = moved(device, half_devices)
        own_wide = widened_at(device)
        partner_rows = fold_rows(widened_at(partner_dev)[:, tile_side - 3:], flags_all[partner_dev])
        links = links_all[device]
        extended = extend(own_wide, links, flags_all[device], partner_rows)
        results = lax.map(lambda pair: tile_step(pair[0], pair[1], dw_kernel, norm_gain, w_up, w_down), (extended, masked_cot(device)))
        grad_ext = results[0]
        sums = tuple((r + lax.optimization_barrier(jnp.sum(v, axis=0)) for r, v in zip(running, results[1:])))
        fold_back = fold_rows(grad_ext[:, tile_side + 3:], flags_all[device])
        interior = grad_ext[:, 3:tile_side + 3]
        low_rows = interior[:, :3] + select_slots(grad_ext[:, tile_side + 3:], links[:, 2])
        top_rows = interior[:, tile_side - 3:] + select_slots(grad_ext[:, :3], links[:, 3])
        partial_wide = jnp.concatenate([low_rows, interior[:, 3:tile_side - 3], top_rows], axis=1)
        return (sums, (partial_wide, fold_back))
    start = (jnp.zeros((7, 7, CH), jnp.float32), jnp.zeros((CH,), jnp.float32), jnp.zeros((CH, FFN), jnp.float32), jnp.zeros((FFN, CH), jnp.float32))
    device_ids = jnp.arange(devices, dtype=jnp.int32)
    grad_sums, (partials, fold_backs) = lax.scan(first_pass, start, device_ids)

    def full_wide(device):
        partner_dev = moved(device, half_devices)
        returned = mirror(fold_backs[partner_dev]).astype(jnp.float32)
        base = partials[device]
        flags = flags_all[device]
        top_rows = base[:, tile_side - 3:] + jnp.where((flags == 1)[:, None, None, None], returned[None], 0.0)
        return jnp.concatenate([base[:, :tile_side - 3], top_rows], axis=1)

    def second_pass(running, device):
        own = full_wide(device)
        from_east = full_wide(moved(device, 1))[:, :, :3].astype(jnp.bfloat16)
        from_west = full_wide(moved(device, -1))[:, :, tile_side + 3:].astype(jnp.bfloat16)
        links = links_all[device]
        grad_out = own[:, :, 3:tile_side + 3] + masked_cot(device).astype(jnp.float32)
        left_cols = grad_out[:, :, :3] + select_slots(from_west, links[:, 0]).astype(jnp.float32)
        right_cols = grad_out[:, :, tile_side - 3:] + select_slots(from_east, links[:, 1]).astype(jnp.float32)
        grad_out = jnp.concatenate([left_cols, grad_out[:, :, 3:tile_side - 3], right_cols], axis=2)
        grad_low = grad_out.astype(jnp.bfloat16).reshape(-1, CH)
        grad_state = jnp.dot(grad_low, w_stem.T, preferred_element_type=jnp.float32).astype(jnp.bfloat16)
        grad_state = grad_state.reshape(slot_total, tile_side, tile_side, CIN)
        grad_stem = running + jnp.dot(states[device].reshape(-1, CIN).T, grad_low, preferred_element_type=jnp.float32)
        return (grad_stem, grad_state)
    grad_stem, grad_states = lax.scan(second_pass, jnp.zeros((CIN, CH), jnp.float32), device_ids)
    grad_state = grad_states.reshape(devices * slot_total, tile_side, tile_side, CIN)
    return (grad_state, grad_stem, grad_sums[0], grad_sums[1], grad_sums[2], grad_sums[3])
```

```python
import jax
import jax.numpy as jnp
from jax import lax
from jax.experimental import pallas as pl
from jax.experimental.pallas import tpu as pltpu
from jax.sharding import PartitionSpec as P


epsilon = 1e-06
root_half = 0.7071067811865476
inv_root_two_pi = 0.3989422804014327
SLOTS = 4
SIDE = 32
QROWS = 8
SUB = 16
CW = 192
CP = 256
FF = 768
EW = SIDE + 6
GW = SIDE + 12
NFOLD = 3 * EW
bf16 = jnp.bfloat16
f32 = jnp.float32
VMEM = pl.BlockSpec(memory_space=pltpu.VMEM)
SMEM = pl.BlockSpec(memory_space=pltpu.SMEM)


def call(kernel, outs, specs, scratch=(), flops=0, size=0):
    single = not isinstance(outs, (list, tuple))
    return pl.pallas_call(
        kernel,
        out_shape=outs,
        in_specs=specs,
        out_specs=VMEM if single else [VMEM] * len(outs),
        scratch_shapes=list(scratch),
        compiler_params=pltpu.CompilerParams(vmem_limit_bytes=52 * 1024 * 1024),
        cost_estimate=pl.CostEstimate(flops=flops, bytes_accessed=size, transcendentals=0),
    )


def struct(shape, dtype):
    return jax.ShapeDtypeStruct(shape, dtype)


def dot(a, b):
    return jnp.dot(a, b, preferred_element_type=f32)


def dot_t(a, b):
    return lax.dot_general(a, b, (((0,), (0,)), ((), ())), preferred_element_type=f32)


def iotas():
    row = lax.broadcasted_iota(jnp.int32, (256, 256), 0)
    col = lax.broadcasted_iota(jnp.int32, (256, 256), 1)
    return row, col


def one_hot(mask):
    return jnp.where(mask, 1.0, 0.0).astype(bf16)


def swap_matrix():
    row, col = iotas()
    return one_hot(col == (row & 15) * 16 + (row >> 4))


def by_slot(slot, links_ref, column):
    link = jnp.full_like(slot, -1)
    for n in range(SLOTS):
        link = jnp.where(slot == n, links_ref[n, column], link)
    return link


def side_matrix(links_ref, column):
    row, col = iotas()
    s = row & 15
    link = by_slot(s & 3, links_ref, column)
    target = jnp.where(link >= 0, row - (s & 3) + link, -1)
    return one_hot(col == target)


def south_matrix(links_ref):
    row, col = iotas()
    s = row & 15
    link = by_slot(s & 3, links_ref, 2)
    target = jnp.where(s >= 4, row - 4, jnp.where(link >= 0, row - s + 12 + link, -1))
    return one_hot(col == target)


def north_matrix(links_ref):
    row, col = iotas()
    s = row & 15
    link = by_slot(s & 3, links_ref, 3)
    target = jnp.where(s < 12, row + 4, jnp.where(link >= 0, row - s + link, -1))
    return one_hot(col == target)


def starts(count):
    return [min(16 * n, count - 16) for n in range(-(-count // 16))]


def picked(matrix, block):
    return dot(matrix, block.reshape(256, CP)).astype(bf16).reshape(16, SUB, CP)


def fold_mask(flags_ref, shape):
    s = lax.broadcasted_iota(jnp.int32, shape, len(shape) - 2)
    mask = jnp.zeros(shape, jnp.int32)
    for n in range(SLOTS):
        mask = jnp.where(s == 12 + n, flags_ref[n], mask)
    return mask == 1


def fold_spread(flags_ref, start):
    row = lax.broadcasted_iota(jnp.int32, (256, 128), 0)
    col = lax.broadcasted_iota(jnp.int32, (256, 128), 1)
    s = row & 15
    flag = jnp.zeros_like(s)
    for n in range(SLOTS):
        flag = jnp.where(s == 12 + n, flags_ref[n], flag)
    return one_hot((flag == 1) & (col == NFOLD - 1 - start - (row >> 4)))


def conv_full(src, base, width, count, kf_ref, lanes, flip):
    total = jnp.zeros((count, 2, 8, 128), f32)
    for a in range(7):
        x = src[pl.ds(base + a * width, count + 6), :, lanes].astype(f32)
        x = x.reshape(count + 6, 2, 8, 128)
        for b in range(7):
            tap = (6 - a) * 7 + 6 - b if flip else a * 7 + b
            total = total + x[b : b + count] * kf_ref[tap, :, lanes]
    return total.reshape(count, SUB, 128)


def gelu_parts(hidden):
    cdf = 0.5 + 0.5 * lax.erf(hidden * root_half)
    bell = jnp.exp(-0.5 * hidden * hidden) * inv_root_two_pi
    return cdf, cdf + hidden * bell


def stem_kernel(state_ref, w_ref, stem_ref, first_ref, last_ref):
    swap = swap_matrix()
    w = w_ref[...]

    def visit(r, carry):
        for h in range(2):
            slabs = [
                state_ref[s & 3, (s >> 2) * QROWS + r, 16 * h : 16 * h + 16, :] for s in range(SUB)
            ]
            x = jnp.concatenate(slabs, axis=0)
            stem = dot(x, w).astype(bf16)
            stem = dot(swap, stem).astype(bf16).reshape(16, SUB, CP)
            stem_ref[r, 16 * h : 16 * h + 16] = stem
            if h == 0:
                first_ref[r] = stem[:3]
            else:
                last_ref[r] = stem[13:]
        return carry

    lax.fori_loop(0, QROWS, visit, 0)


def cot_kernel(cot_ref, wet_ref, out_ref):
    swap = swap_matrix()

    def visit(r, carry):
        for h in range(2):
            slabs = []
            for s in range(SUB):
                slab = cot_ref[s & 3, (s >> 2) * QROWS + r, 16 * h : 16 * h + 16, :]
                slabs.append(jnp.where((s & 3) < wet_ref[0], slab, jnp.zeros_like(slab)))
            x = jnp.concatenate(slabs, axis=0)
            out_ref[r, 16 * h : 16 * h + 16] = dot(swap, x).astype(bf16).reshape(16, SUB, CW)
        return carry

    lax.fori_loop(0, QROWS, visit, 0)


def widen_kernel(west_ref, east_ref, top_ref, links_ref, flags_ref, w_out, e_out, fold_out, rows):
    for source, column, out in ((west_ref, 0, w_out), (east_ref, 1, e_out)):
        matrix = side_matrix(links_ref, column)
        for start in starts(24):
            out[start : start + 16] = picked(matrix, source[start : start + 16])
    mask = fold_mask(flags_ref, (1, SUB, CP))
    rows[...] = jnp.zeros_like(rows)

    def chosen(block):
        return jnp.sum(jnp.where(mask, block.astype(f32), 0.0), axis=1)

    for k in range(3):
        rows[k * EW : k * EW + 3] = chosen(w_out[(5 + k) * 3 : (6 + k) * 3])
        rows[k * EW + 3 : k * EW + 35] = chosen(top_ref[k])
        rows[k * EW + 35 : k * EW + 38] = chosen(e_out[(5 + k) * 3 : (6 + k) * 3])
    fold_out[...] = rows[...].astype(bf16)


def fill_halo(ref, width, links_ref):
    south = south_matrix(links_ref)
    north = north_matrix(links_ref)
    for start in starts(3 * width):
        ref[start : start + 16] = picked(south, ref[8 * width + start : 8 * width + start + 16])
        top = 11 * width + start
        ref[top : top + 16] = picked(north, ref[3 * width + start : 3 * width + start + 16])


def conv_block(src, base, width, count, kb_ref, lanes, flip):
    total = jnp.zeros((count, SUB, 128), f32)
    for a in range(7):
        x = src[pl.ds(base + a * width, count + 6), :, lanes]
        part = None
        for b in range(7):
            tap = (6 - a) * 7 + 6 - b if flip else a * 7 + b
            term = x[b : b + count] * kb_ref[tap, :, lanes]
            part = term if part is None else part + term
        total = total + part.astype(f32)
    return total


def front_kernel(
    stem_ref,
    w_ref,
    e_ref,
    partner_ref,
    cot_ref,
    kb_ref,
    kf_ref,
    gain_ref,
    up_ref,
    up_t_ref,
    down_t_ref,
    links_ref,
    flags_ref,
    ext_ref,
    gm_ref,
    gup_ref,
    gdown_ref,
    ggain_ref,
    back_ref,
    mixed_ref,
    rows_ref,
):
    for r in range(QROWS):
        base = (r + 3) * EW
        ext_ref[base : base + 3] = w_ref[3 * r : 3 * r + 3]
        ext_ref[base + 3 : base + 35] = stem_ref[r]
        ext_ref[base + 35 : base + 38] = e_ref[3 * r : 3 * r + 3]
    fill_halo(ext_ref, EW, links_ref)
    partner = partner_ref[...]
    for start in starts(NFOLD):
        top = 11 * EW + start
        add = dot(fold_spread(flags_ref, start), partner).astype(bf16).reshape(16, SUB, CP)
        mask = fold_mask(flags_ref, (1, SUB, CP))
        ext_ref[top : top + 16] = jnp.where(mask, add, ext_ref[top : top + 16])
    gm_ref[...] = jnp.zeros_like(gm_ref)
    gup_ref[...] = jnp.zeros_like(gup_ref)
    gdown_ref[...] = jnp.zeros_like(gdown_ref)
    ggain_ref[...] = jnp.zeros_like(ggain_ref)

    def visit(r, carry):
        for half in range(2):
            lanes = slice(128 * half, 128 * half + 128)
            for block in range(4):
                mixed_ref[8 * block : 8 * block + 8, :, lanes] = conv_full(
                    ext_ref, r * EW + 8 * block, EW, 8, kf_ref, lanes, False
                )
        mixed = mixed_ref[...].reshape(512, CP)
        lane = lax.broadcasted_iota(jnp.int32, (1, CP), 1)
        average = jnp.sum(mixed, axis=-1, keepdims=True) * (1.0 / CW)
        centred = jnp.where(lane < CW, mixed - average, 0.0)
        variance = jnp.sum(centred * centred, axis=-1, keepdims=True) * (1.0 / CW)
        inv_std = lax.rsqrt(variance + epsilon)
        normed = centred * inv_std
        gain = gain_ref[...]
        low = (normed * gain).astype(bf16)
        cot = cot_ref[r].reshape(512, CW)
        grad_normed = jnp.zeros((512, CP), f32)
        for c in range(3):
            cols = slice(256 * c, 256 * c + 256)
            hidden = dot(low, up_ref[:, cols])
            grad_act = dot(cot, down_t_ref[:, cols])
            cdf, slope = gelu_parts(hidden)
            act = (hidden * cdf).astype(bf16)
            grad_hidden = (grad_act * slope).astype(bf16)
            gdown_ref[:, cols] += dot_t(cot, act)
            gup_ref[:, cols] += dot_t(low, grad_hidden)
            grad_normed = grad_normed + dot(grad_hidden, up_t_ref[cols, :])
        product = grad_normed * normed
        ggain_ref[...] += jnp.sum(product.reshape(64, 8, CP), axis=0)
        grad_unit = grad_normed * gain
        mean_unit = jnp.sum(grad_unit, axis=-1, keepdims=True) * (1.0 / CW)
        mean_both = jnp.sum(product * gain, axis=-1, keepdims=True) * (1.0 / CW)
        grad_mixed = inv_std * (grad_unit - mean_unit - normed * mean_both)
        gm_ref[pl.ds(r * GW + 6, SIDE)] = grad_mixed.astype(bf16).reshape(SIDE, SUB, CP)
        return carry

    lax.fori_loop(0, QROWS, visit, 0)
    rows_ref[...] = jnp.zeros_like(rows_ref)
    mask = fold_mask(flags_ref, (1, SUB, 128))
    for t in range(3):
        for half in range(2):
            lanes = slice(128 * half, 128 * half + 128)
            for q in range(0, EW, 8):
                count = min(8, EW - q)
                total = jnp.zeros((count, SUB, 128), f32)
                for a in range(4 + t, 7):
                    x = gm_ref[(11 + t - a) * GW + q : (11 + t - a) * GW + q + count + 6, :, lanes]
                    part = None
                    for b in range(7):
                        term = x[6 - b : 6 - b + count] * kb_ref[a * 7 + b, :, lanes]
                        part = term if part is None else part + term
                    total = total + part.astype(f32)
                rows_ref[t * EW + q : t * EW + q + count, lanes] = jnp.sum(
                    jnp.where(mask, total, 0.0), axis=1
                )
    back_ref[...] = rows_ref[...].astype(bf16)


def taps_kernel(ext_ref, gm_ref, out_ref, acc_ref):
    acc_ref[...] = jnp.zeros_like(acc_ref)

    def visit(r, carry):
        for half in range(2):
            lanes = slice(128 * half, 128 * half + 128)
            for a in range(7):
                sums = [jnp.zeros((2, 8, 128), f32) for _ in range(7)]
                for block in range(4):
                    x = ext_ref[pl.ds((r + a) * EW + 8 * block, 14), :, lanes].astype(f32)
                    g = gm_ref[pl.ds(r * GW + 6 + 8 * block, 8), :, lanes].astype(f32)
                    x = x.reshape(14, 2, 8, 128)
                    g = g.reshape(8, 2, 8, 128)
                    for b in range(7):
                        for n in range(8):
                            sums[b] = sums[b] + x[b + n] * g[n]
                for b in range(7):
                    acc_ref[a * 7 + b, :, lanes] += sums[b].reshape(SUB, 128)
        return carry

    lax.fori_loop(0, QROWS, visit, 0)
    out_ref[...] = jnp.sum(acc_ref[...], axis=1)


def back_kernel(gm_ref, kf_ref, partner_ref, links_ref, flags_ref, mid_ref, w_ref, e_ref, gmx, row):
    gmx[0 : 3 * GW] = jnp.zeros((3 * GW, SUB, CP), bf16)
    gmx[3 * GW : 11 * GW] = gm_ref[...]
    gmx[11 * GW : 14 * GW] = jnp.zeros((3 * GW, SUB, CP), bf16)
    fill_halo(gmx, GW, links_ref)

    def visit(r, carry):
        for half in range(2):
            lanes = slice(128 * half, 128 * half + 128)
            for q in range(0, EW, 8):
                count = min(8, EW - q)
                row[r, q : q + count, :, lanes] = conv_full(
                    gmx, r * GW + q, GW, count, kf_ref, lanes, True
                )
        return carry

    lax.fori_loop(0, QROWS, visit, 0)
    partner = partner_ref[...]
    for k in range(3):
        for q in (0, 16, EW - 16):
            skip = 10 if q == EW - 16 else 0
            add = dot(fold_spread(flags_ref, k * EW + q), partner).reshape(16, SUB, CP)
            row[5 + k, q + skip : q + 16] += add[skip:]
    for r in range(QROWS):
        mid_ref[r] = row[r, 3:35]
        w_ref[3 * r : 3 * r + 3] = row[r, 0:3].astype(bf16)
        e_ref[3 * r : 3 * r + 3] = row[r, 35:38].astype(bf16)


def final_kernel(
    mid_ref, cot_ref, w_ref, e_ref, state_ref, stem_t_ref, links_ref, out_ref, gstem_ref, gout
):
    swap = swap_matrix()
    gout[...] = mid_ref[...]
    gout[:, :, :, 0:CW] = gout[:, :, :, 0:CW] + cot_ref[...].astype(f32)
    for source, column, at in ((w_ref, 0, 0), (e_ref, 1, 29)):
        matrix = side_matrix(links_ref, column)
        for start in starts(24):
            got = dot(matrix, source[start : start + 16].reshape(256, CP)).reshape(16, SUB, CP)
            for n in range(16):
                if start == 8 and n < 8:
                    continue
                r, j = divmod(start + n, 3)
                gout[r, at + j] += got[n]
    gstem_ref[...] = jnp.zeros_like(gstem_ref)

    def visit(r, carry):
        for h in range(2):
            low = gout[r, 16 * h : 16 * h + 16].astype(bf16).reshape(256, CP)
            low = dot(swap, low).astype(bf16)
            slabs = [
                state_ref[s & 3, (s >> 2) * QROWS + r, 16 * h : 16 * h + 16, :] for s in range(SUB)
            ]
            gstem_ref[...] += dot_t(jnp.concatenate(slabs, axis=0), low)
            grad = dot(low, stem_t_ref[...]).astype(bf16)
            for s in range(SUB):
                out_ref[s & 3, (s >> 2) * QROWS + r, 16 * h : 16 * h + 16, :] = grad[
                    16 * s : 16 * s + 16
                ]
        return carry

    lax.fori_loop(0, QROWS, visit, 0)


def shifted(block, distance):
    count = lax.axis_size("tiles")
    return lax.ppermute(block, "tiles", [((i - distance) % count, i) for i in range(count)])


def levels():
    left, stride, out = lax.axis_size("tiles"), 1, []
    while left > 1:
        size = 2 if stride == 1 or left % 4 else 4
        out.append((stride, size))
        stride, left = stride * size, left // size
    return out


def rotated(block, level, distance):
    stride, size = level
    route = []
    for i in range(lax.axis_size("tiles")):
        place = (i // stride) % size
        route.append((i, i + ((place + distance) % size - place) * stride))
    return lax.ppermute(block, "tiles", route)


def place_in(level):
    stride, size = level
    return (lax.axis_index("tiles") // stride) % size


def tree_sum(terms):
    while len(terms) > 1:
        half = len(terms) // 2
        terms = [terms[n] + terms[n + half] for n in range(half)]
    return terms[0]


def scatter_sum(block, level):
    size = level[1]
    rows = block.shape[0] // size
    me = place_in(level)

    def piece(distance):
        return lax.dynamic_slice_in_dim(block, ((me + distance) % size) * rows, rows, 0)

    terms = [piece(0)] + [rotated(piece(n), level, n) for n in range(1, size)]
    return tree_sum([t.astype(f32) for t in terms]).astype(bf16)


def full_sum(block, level):
    terms = [block] + [rotated(block, level, n) for n in range(1, level[1])]
    return tree_sum([t.astype(f32) for t in terms])


def gathered(block, level):
    size = level[1]
    rows = block.shape[0]
    me = place_in(level)
    out = jnp.zeros((rows * size,) + block.shape[1:], block.dtype)
    for n in range(size):
        part = rotated(block, level, n) if n else block
        out = lax.dynamic_update_slice_in_dim(out, part, ((me - n) % size) * rows, 0)
    return out


def body(
    ocean_state,
    cotangent,
    w_stem,
    dw_kernel,
    norm_gain,
    w_up,
    w_down,
    tile_links,
    fold_flags,
    wet_count,
):
    cin = ocean_state.shape[3]
    half_way = lax.axis_size("tiles") // 2
    pad = CP - CW
    stem_w = jnp.pad(w_stem, ((0, 0), (0, pad)))
    kb = jnp.pad(dw_kernel.reshape(49, 1, CW), ((0, 0), (0, 0), (0, pad)))
    kf = jnp.broadcast_to(kb.astype(f32), (49, 8, CP))
    kb = jnp.broadcast_to(kb, (49, SUB, CP))
    gain = jnp.pad(norm_gain, (0, pad))[None]
    up = jnp.pad(w_up, ((0, pad), (0, 0)))
    down_t = w_down.T

    stem, first, last = call(
        stem_kernel,
        [
            struct((QROWS, SIDE, SUB, CP), bf16),
            struct((QROWS, 3, SUB, CP), bf16),
            struct((QROWS, 3, SUB, CP), bf16),
        ],
        [VMEM, VMEM],
    )(ocean_state, stem_w)
    from_west = shifted(last, 1).reshape(24, SUB, CP)
    from_east = shifted(first, -1).reshape(24, SUB, CP)
    cot = call(cot_kernel, struct((QROWS, SIDE, SUB, CW), bf16), [VMEM, SMEM])(cotangent, wet_count)
    west, east, fold = call(
        widen_kernel,
        [struct((24, SUB, CP), bf16), struct((24, SUB, CP), bf16), struct((128, CP), bf16)],
        [VMEM, VMEM, VMEM, SMEM, SMEM],
        [pltpu.VMEM((128, CP), f32)],
    )(from_west, from_east, stem[5:8], tile_links, fold_flags)
    partner = shifted(fold, half_way)
    ext, gm, gup, gdown, ggain, back = call(
        front_kernel,
        [
            struct((14 * EW, SUB, CP), bf16),
            struct((QROWS * GW, SUB, CP), bf16),
            struct((CP, FF), f32),
            struct((CW, FF), f32),
            struct((8, CP), f32),
            struct((128, CP), bf16),
        ],
        [VMEM] * 11 + [SMEM, SMEM],
        [pltpu.VMEM((SIDE, SUB, CP), f32), pltpu.VMEM((128, CP), f32)],
    )(stem, west, east, partner, cot, kb, kf, gain, up, up.T, down_t, tile_links, fold_flags)
    parts = [g[:CW, 256 * c : 256 * c + 256] for g in (gup, gdown) for c in range(3)]
    big = jnp.concatenate(parts, axis=0).astype(bf16)
    plan = levels()
    for level in plan[:3]:
        big = scatter_sum(big, level)
    for level in plan[3:]:
        big = full_sum(big, level).astype(bf16)
    partner_back = shifted(back, half_way)
    gkernel = call(
        taps_kernel, struct((49, CP), f32), [VMEM, VMEM], [pltpu.VMEM((49, SUB, CP), f32)]
    )(ext, gm)
    mid, back_w, back_e = call(
        back_kernel,
        [
            struct((QROWS, SIDE, SUB, CP), f32),
            struct((24, SUB, CP), bf16),
            struct((24, SUB, CP), bf16),
        ],
        [VMEM, VMEM, VMEM, SMEM, SMEM],
        [pltpu.VMEM((14 * GW, SUB, CP), bf16), pltpu.VMEM((QROWS, EW, SUB, CP), f32)],
    )(gm, kf, partner_back, tile_links, fold_flags)
    back_from_west = shifted(back_e, 1)
    back_from_east = shifted(back_w, -1)
    grad_state, gstem = call(
        final_kernel,
        [struct(ocean_state.shape, bf16), struct((cin, CP), f32)],
        [VMEM] * 6 + [SMEM],
        [pltpu.VMEM((QROWS, SIDE, SUB, CP), f32)],
    )(mid, cot, back_from_west, back_from_east, ocean_state, stem_w.T, tile_links)
    rest = jnp.concatenate(
        [gstem, gkernel, jnp.sum(ggain, axis=0, keepdims=True), jnp.zeros((15, CP), f32)], axis=0
    )
    for level in plan:
        rest = full_sum(rest.astype(bf16), level)
    for level in plan[2::-1]:
        big = gathered(big, level)
    big = big.astype(f32).reshape(2, 3, CW, CP)
    gup = jnp.concatenate([big[0, c] for c in range(3)], axis=1)
    gdown = jnp.concatenate([big[1, c].T for c in range(3)], axis=0)
    gstem, gkernel, ggain = rest[:cin, :CW], rest[cin : cin + 49, :CW], rest[cin + 49, :CW]
    return (grad_state, gstem, gkernel.reshape(7, 7, CW), ggain, gup, gdown)


def solution(mesh):
    return jax.shard_map(
        body,
        mesh=mesh,
        in_specs=(
            P("tiles", None, None, None),
            P("tiles", None, None, None),
            P(),
            P(),
            P(),
            P(),
            P(),
            P("tiles", None),
            P("tiles"),
            P("tiles"),
        ),
        out_specs=(P("tiles", None, None, None), P(), P(), P(), P(), P()),
        check_vma=False,
    )
```

```python
import jax
import jax.numpy as jnp
from jax import lax
from jax.experimental import pallas as pl
from jax.experimental.pallas import tpu as pltpu
from jax.sharding import PartitionSpec as P


epsilon = 1e-06
root_half = 0.7071067811865476
inv_root_two_pi = 0.3989422804014327
SLOTS = 4
SIDE = 32
QROWS = 8
SUB = 16
CW = 192
CP = 256
FF = 768
EW = SIDE + 6
GW = SIDE + 12
EP = EW // 2
GP = GW // 2
GS = SIDE + 16
NFOLD = 3 * EW
bf16 = jnp.bfloat16
f32 = jnp.float32
VMEM = pl.BlockSpec(memory_space=pltpu.VMEM)
SMEM = pl.BlockSpec(memory_space=pltpu.SMEM)


def call(kernel, outs, specs, scratch=(), micros=1):
    single = not isinstance(outs, (list, tuple))
    return pl.pallas_call(
        kernel,
        out_shape=outs,
        in_specs=specs,
        out_specs=VMEM if single else [VMEM] * len(outs),
        scratch_shapes=list(scratch),
        compiler_params=pltpu.CompilerParams(vmem_limit_bytes=52 * 1024 * 1024),
        cost_estimate=pl.CostEstimate(
            flops=micros * 1_150_000_000, bytes_accessed=micros * 1_000_000, transcendentals=0
        ),
    )


def struct(shape, dtype):
    return jax.ShapeDtypeStruct(shape, dtype)


def dot(a, b):
    return jnp.dot(a, b, preferred_element_type=f32)


def dot_t(a, b):
    return lax.dot_general(a, b, (((0,), (0,)), ((), ())), preferred_element_type=f32)


def iotas():
    row = lax.broadcasted_iota(jnp.int32, (256, 256), 0)
    col = lax.broadcasted_iota(jnp.int32, (256, 256), 1)
    return row, col


def one_hot(mask):
    return jnp.where(mask, 1.0, 0.0).astype(bf16)


def swap_matrix():
    row, col = iotas()
    return one_hot(col == (row & 15) * 16 + (row >> 4))


def by_slot(slot, links_ref, column):
    link = jnp.full_like(slot, -1)
    for n in range(SLOTS):
        link = jnp.where(slot == n, links_ref[n, column], link)
    return link


def side_matrix(links_ref, column):
    row, col = iotas()
    s = row & 15
    link = by_slot(s & 3, links_ref, column)
    target = jnp.where(link >= 0, row - (s & 3) + link, -1)
    return one_hot(col == target)


def south_matrix(links_ref):
    row, col = iotas()
    s = row & 15
    link = by_slot(s & 3, links_ref, 2)
    target = jnp.where(s >= 4, row - 4, jnp.where(link >= 0, row - s + 12 + link, -1))
    return one_hot(col == target)


def north_matrix(links_ref):
    row, col = iotas()
    s = row & 15
    link = by_slot(s & 3, links_ref, 3)
    target = jnp.where(s < 12, row + 4, jnp.where(link >= 0, row - s + link, -1))
    return one_hot(col == target)


def starts(count):
    return [min(16 * n, count - 16) for n in range(-(-count // 16))]


def picked(matrix, block):
    lanes = block.shape[-1]
    return dot(matrix, block.reshape(256, lanes)).astype(bf16).reshape(16, SUB, lanes)


def fold_mask(flags_ref, shape):
    s = lax.broadcasted_iota(jnp.int32, shape, len(shape) - 2)
    mask = jnp.zeros(shape, jnp.int32)
    for n in range(SLOTS):
        mask = jnp.where(s == 12 + n, flags_ref[n], mask)
    return mask == 1


def fold_spread(flags_ref, start, step=1, parity=0):
    row = lax.broadcasted_iota(jnp.int32, (256, 128), 0)
    col = lax.broadcasted_iota(jnp.int32, (256, 128), 1)
    s = row & 15
    flag = jnp.zeros_like(s)
    for n in range(SLOTS):
        flag = jnp.where(s == 12 + n, flags_ref[n], flag)
    return one_hot((flag == 1) & (col == NFOLD - 1 - parity - step * (start + (row >> 4))))


def tap_of(a, b, flip):
    return (6 - a) * 7 + 6 - b if flip else a * 7 + b


def pair_weights(diag_ref, a, flip):
    def block(b):
        if 0 <= b <= 6:
            return diag_ref[tap_of(a, b, flip)]
        return jnp.zeros((128, 128), bf16)

    rows = [jnp.concatenate([block(m), block(m - 1)], axis=1) for m in range(8)]
    return jnp.concatenate(rows, axis=0)


def pair_term(src, bases, count, diag_ref, a, flip):
    parts = []
    for n in range(4):
        at = [src[pl.ds(base + n, count)].reshape(count * SUB, CP) for base in bases]
        parts.append(jnp.concatenate(at, axis=0))
    return dot(jnp.concatenate(parts, axis=1), pair_weights(diag_ref, a, flip))


def conv_pairs(src, base, width, count, diag_ref, flip):
    total = None
    for a in range(7):
        term = pair_term(src, [base + a * width], count, diag_ref, a, flip)
        total = term if total is None else total + term
    return total


def conv_rest(src, base, width, count, kf_ref, flip):
    total = jnp.zeros((count, 2, 8, 128), f32)
    for a in range(7):
        x = src[pl.ds(base + a * width, count + 6)].astype(f32).reshape(count + 6, 2, 8, 128)
        for b in range(7):
            total = total + x[b : b + count] * kf_ref[tap_of(a, b, flip), :, 128:]
    return total.reshape(count, SUB, 128)


def gelu_parts(hidden):
    cdf = 0.5 + 0.5 * lax.erf(hidden * root_half)
    bell = jnp.exp(-0.5 * hidden * hidden) * inv_root_two_pi
    return cdf, cdf + hidden * bell


def stem_kernel(state_ref, w_ref, stem_ref, moved_ref, first_ref, last_ref):
    swap = swap_matrix()
    w = w_ref[...]

    def visit(r, carry):
        for h in range(2):
            slabs = [
                state_ref[s & 3, (s >> 2) * QROWS + r, 16 * h : 16 * h + 16, :] for s in range(SUB)
            ]
            x = dot(swap, jnp.concatenate(slabs, axis=0)).astype(bf16)
            stem_ref[r, 16 * h : 16 * h + 16] = dot(x, w).astype(bf16).reshape(16, SUB, CP)
            x = x.reshape(16, SUB, -1)
            moved_ref[r, 16 * h : 16 * h + 16] = x
            if h == 0:
                first_ref[r] = x[:3]
            else:
                last_ref[r] = x[13:]
        return carry

    lax.fori_loop(0, QROWS, visit, 0)


def cot_kernel(cot_ref, wet_ref, out_ref):
    swap = swap_matrix()

    def visit(r, carry):
        for h in range(2):
            slabs = []
            for s in range(SUB):
                slab = cot_ref[s & 3, (s >> 2) * QROWS + r, 16 * h : 16 * h + 16, :]
                slabs.append(jnp.where((s & 3) < wet_ref[0], slab, jnp.zeros_like(slab)))
            x = jnp.concatenate(slabs, axis=0)
            out_ref[r, 16 * h : 16 * h + 16] = dot(swap, x).astype(bf16).reshape(16, SUB, CW)
        return carry

    lax.fori_loop(0, QROWS, visit, 0)


def widen_kernel(
    west_ref,
    east_ref,
    stem_ref,
    stem_w_ref,
    links_ref,
    flags_ref,
    ws_out,
    es_out,
    w_out,
    e_out,
    fold_out,
    rows,
):
    for source, column, raw, out in (
        (west_ref, 0, ws_out, w_out),
        (east_ref, 1, es_out, e_out),
    ):
        matrix = side_matrix(links_ref, column)
        for start in starts(24):
            got = picked(matrix, source[start : start + 16])
            raw[start : start + 16] = got
            got = dot(got.reshape(256, -1), stem_w_ref[...]).astype(bf16)
            out[start : start + 16] = got.reshape(16, SUB, CP)
    mask = fold_mask(flags_ref, (1, SUB, CP))
    rows[...] = jnp.zeros_like(rows)

    def chosen(block):
        return jnp.sum(jnp.where(mask, block.astype(f32), 0.0), axis=1)

    for k in range(3):
        rows[k * EW : k * EW + 3] = chosen(w_out[(5 + k) * 3 : (6 + k) * 3])
        rows[k * EW + 3 : k * EW + 35] = chosen(stem_ref[5 + k])
        rows[k * EW + 35 : k * EW + 38] = chosen(e_out[(5 + k) * 3 : (6 + k) * 3])
    fold_out[...] = rows[...].astype(bf16)


def fill_halo(ref, width, links_ref):
    south = south_matrix(links_ref)
    north = north_matrix(links_ref)
    for start in starts(3 * width):
        ref[start : start + 16] = picked(south, ref[8 * width + start : 8 * width + start + 16])
        top = 11 * width + start
        ref[top : top + 16] = picked(north, ref[3 * width + start : 3 * width + start + 16])


def front_kernel(
    stem_ref,
    w_ref,
    e_ref,
    partner_ref,
    cot_ref,
    diag_ref,
    kf_ref,
    gain_ref,
    up_ref,
    up_t_ref,
    down_t_ref,
    links_ref,
    flags_ref,
    ext0_ref,
    ext1_ref,
    gm0_ref,
    gm1_ref,
    gup_ref,
    gdown_ref,
    ggain_ref,
    back_ref,
    mixed_ref,
    chosen_ref,
    rows_ref,
):
    for r in range(QROWS):
        west, east = w_ref[3 * r : 3 * r + 3], e_ref[3 * r : 3 * r + 3]
        x = jnp.concatenate([west, stem_ref[r], east], axis=0)
        pairs = x[:, :, :128].reshape(EP, 2, SUB, 128)
        ext0_ref[(r + 3) * EP : (r + 4) * EP, :, :128] = pairs[:, 0]
        ext0_ref[(r + 3) * EP : (r + 4) * EP, :, 128:] = pairs[:, 1]
        ext1_ref[(r + 3) * EW : (r + 4) * EW] = x[:, :, 128:]
    fill_halo(ext0_ref, EP, links_ref)
    fill_halo(ext1_ref, EW, links_ref)
    partner = partner_ref[...]
    mask = fold_mask(flags_ref, (1, SUB, CP))
    for start in starts(3 * EP):
        top = 11 * EP + start
        halves = [dot(fold_spread(flags_ref, start, 2, n), partner[:, :128]) for n in range(2)]
        add = jnp.concatenate(halves, axis=1).astype(bf16).reshape(16, SUB, CP)
        ext0_ref[top : top + 16] = jnp.where(mask, add, ext0_ref[top : top + 16])
    for start in starts(NFOLD):
        top = 11 * EW + start
        add = dot(fold_spread(flags_ref, start), partner[:, 128:]).astype(bf16)
        ext1_ref[top : top + 16] = jnp.where(
            mask[:, :, :128], add.reshape(16, SUB, 128), ext1_ref[top : top + 16]
        )
    gm0_ref[...] = jnp.zeros_like(gm0_ref)
    gm1_ref[...] = jnp.zeros_like(gm1_ref)
    gup_ref[...] = jnp.zeros_like(gup_ref)
    gdown_ref[...] = jnp.zeros_like(gdown_ref)
    ggain_ref[...] = jnp.zeros_like(ggain_ref)
    chosen_ref[...] = jnp.zeros_like(chosen_ref)

    mixed_ref[:, :, :, :, :128] = jnp.zeros((QROWS, 16, 2, SUB, 128), f32)

    def mix_rest(r):
        for block in range(4):
            mixed_ref[r, 4 * block : 4 * block + 4, :, :, 128:] = conv_rest(
                ext1_ref, r * EW + 8 * block, EW, 8, kf_ref, False
            ).reshape(4, 2, SUB, 128)

    def mix(a, carry):
        for r in (0, 4):
            got = pair_term(ext0_ref, [(r + k + a) * EP for k in range(4)], 16, diag_ref, a, False)
            for n in range(2):
                half = got[:, 128 * n : 128 * n + 128].reshape(4, 16, SUB, 128)
                mixed_ref[r : r + 4, :, n, :, :128] += half
        mix_rest(a)
        return carry

    lax.fori_loop(0, 7, mix, 0)
    mix_rest(7)

    def visit(r, carry):
        mixed = mixed_ref[r].reshape(512, CP)
        lane = lax.broadcasted_iota(jnp.int32, (1, CP), 1)
        average = jnp.sum(mixed, axis=-1, keepdims=True) * (1.0 / CW)
        centred = jnp.where(lane < CW, mixed - average, 0.0)
        variance = jnp.sum(centred * centred, axis=-1, keepdims=True) * (1.0 / CW)
        inv_std = lax.rsqrt(variance + epsilon)
        normed = centred * inv_std
        gain = gain_ref[...]
        low = (normed * gain).astype(bf16)
        cot = cot_ref[r].reshape(512, CW)
        grad_normed = jnp.zeros((512, CP), f32)
        for c in range(3):
            cols = slice(256 * c, 256 * c + 256)
            hidden = dot(low, up_ref[:, cols])
            grad_act = dot(cot, down_t_ref[:, cols])
            cdf, slope = gelu_parts(hidden)
            act = (hidden * cdf).astype(bf16)
            grad_hidden = (grad_act * slope).astype(bf16)
            gdown_ref[:, cols] += dot_t(cot, act)
            gup_ref[:, cols] += dot_t(low, grad_hidden)
            grad_normed = grad_normed + dot(grad_hidden, up_t_ref[cols, :])
        product = grad_normed * normed
        ggain_ref[...] += jnp.sum(product.reshape(64, 8, CP), axis=0)
        grad_unit = grad_normed * gain
        mean_unit = jnp.sum(grad_unit, axis=-1, keepdims=True) * (1.0 / CW)
        mean_both = jnp.sum(product * gain, axis=-1, keepdims=True) * (1.0 / CW)
        grad_mixed = inv_std * (grad_unit - mean_unit - normed * mean_both)
        slots = grad_mixed.reshape(SIDE, SUB, CP)
        chosen_ref[pl.ds(r * GS + 8, SIDE)] = jnp.sum(jnp.where(mask, slots, 0.0), axis=1)
        low_mixed = slots.astype(bf16)
        pairs = low_mixed[:, :, :128].reshape(16, 2, SUB, 128)
        gm0_ref[pl.ds(r * GP + 3, 16), :, :128] = pairs[:, 0]
        gm0_ref[pl.ds(r * GP + 3, 16), :, 128:] = pairs[:, 1]
        gm1_ref[pl.ds(r * GW + 6, SIDE)] = low_mixed[:, :, 128:]
        return carry

    lax.fori_loop(0, QROWS, visit, 0)
    rows_ref[...] = jnp.zeros_like(rows_ref)
    for t in range(3):
        total = jnp.zeros((EW, CP), f32)
        for a in range(4 + t, 7):
            x = chosen_ref[(11 + t - a) * GS : (12 + t - a) * GS]
            for b in range(7):
                total = total + x[8 - b : 8 - b + EW] * kf_ref[a * 7 + b, 0:1, :]
        rows_ref[t * EW : t * EW + EW] = total
    back_ref[...] = rows_ref[...].astype(bf16)


def taps_kernel(ext0_ref, ext1_ref, gm0_ref, gm1_ref, out_ref, acc_ref, turned_ref):
    acc_ref[...] = jnp.zeros_like(acc_ref)
    for r in range(QROWS):
        g = gm0_ref[r * GP + 3 : r * GP + 19].reshape(256, CP)
        turned_ref[:, 256 * r : 256 * r + 256] = g.T
    row = lax.broadcasted_iota(jnp.int32, (128, 128), 0)
    col = lax.broadcasted_iota(jnp.int32, (128, 128), 1)
    diagonal = row == col

    def visit(a, carry):
        turned = turned_ref[...]
        sums = [jnp.zeros((8, 128), f32) for _ in range(7)]
        for n in range(4):
            at = [ext0_ref[pl.ds((r + a) * EP + n, 16)].reshape(256, CP) for r in range(QROWS)]
            both = dot(turned, jnp.concatenate(at, axis=0))
            for out_col in range(2):
                for in_col in range(2):
                    b = 2 * n + in_col - out_col
                    if 0 <= b <= 6:
                        part = both[
                            128 * out_col : 128 * out_col + 128, 128 * in_col : 128 * in_col + 128
                        ]
                        part = jnp.where(diagonal, part, 0.0).reshape(16, 8, 128)
                        sums[b] = sums[b] + jnp.sum(part, axis=0)
        for b in range(7):
            acc_ref[a * 7 + b, :, :128] += sums[b]
        rest = [jnp.zeros((2, 8, 128), f32) for _ in range(7)]
        for r in range(QROWS):
            for block in range(4):
                x = ext1_ref[pl.ds((r + a) * EW + 8 * block, 14)].astype(f32)
                g = gm1_ref[r * GW + 6 + 8 * block : r * GW + 14 + 8 * block].astype(f32)
                x = x.reshape(14, 2, 8, 128)
                g = g.reshape(8, 2, 8, 128)
                for b in range(7):
                    for n in range(8):
                        rest[b] = rest[b] + x[b + n] * g[n]
        for b in range(7):
            acc_ref[a * 7 + b, :, 128:] += rest[b][0] + rest[b][1]
        return carry

    lax.fori_loop(0, 7, visit, 0)
    out_ref[...] = jnp.sum(acc_ref[...], axis=1)


def back_kernel(
    gm0_ref,
    gm1_ref,
    diag_ref,
    kf_ref,
    partner_ref,
    cot_ref,
    moved_ref,
    ws_ref,
    es_ref,
    links_ref,
    flags_ref,
    after_ref,
    mid_ref,
    w_ref,
    e_ref,
    gstem_ref,
    gmx0,
    gmx1,
    row,
):
    for source, target, width in ((gm0_ref, gmx0, GP), (gm1_ref, gmx1, GW)):
        edge = jnp.zeros((3 * width, SUB, target.shape[-1]), bf16)
        target[0 : 3 * width] = edge
        target[3 * width : 11 * width] = source[...]
        target[11 * width : 14 * width] = edge
        fill_halo(target, width, links_ref)

    def visit(r, carry):
        pairs = conv_pairs(gmx0, r * GP, GP, EP, diag_ref, True)
        for n in range(2):
            row[r, :, n, :, :128] = pairs[:, 128 * n : 128 * n + 128].reshape(EP, SUB, 128)
        for q in range(0, EW, 8):
            count = min(8, EW - q)
            row[r, q // 2 : (q + count) // 2, :, :, 128:] = conv_rest(
                gmx1, r * GW + q, GW, count, kf_ref, True
            ).reshape(count // 2, 2, SUB, 128)
        return carry

    lax.fori_loop(0, QROWS, visit, 0)
    partner = partner_ref[...]
    for k in range(3):
        for q in (0, 16, EW - 16):
            skip = 10 if q == EW - 16 else 0
            add = dot(fold_spread(flags_ref, k * EW + q), partner).reshape(16, SUB, CP)
            row[5 + k, (q + skip) // 2 : q // 2 + 8] += add[skip:].reshape(-1, 2, SUB, CP)
    for r in range(QROWS):
        full = row[r].reshape(EW, SUB, CP)
        mid_ref[r] = full[3:35]
        w_ref[3 * r : 3 * r + 3] = full[0:3].astype(bf16)
        e_ref[3 * r : 3 * r + 3] = full[35:38].astype(bf16)
    cin = moved_ref.shape[-1]
    gstem = dot_t(ws_ref[...].reshape(24 * SUB, cin), w_ref[...].reshape(24 * SUB, CP))
    gstem += dot_t(es_ref[...].reshape(24 * SUB, cin), e_ref[...].reshape(24 * SUB, CP))
    gstem_ref[...] = gstem
    for r in range(QROWS):
        own = mid_ref[r, :, :, :CW] + cot_ref[r].astype(f32)
        own = own.astype(bf16).reshape(SIDE * SUB, CW)
        gstem_ref[:, :CW] += dot_t(moved_ref[r].reshape(SIDE * SUB, cin), own)


def final_kernel(
    mid_ref, cot_ref, w_ref, e_ref, stem_t_ref, links_ref, out_ref, gout
):
    swap = swap_matrix()
    gout[...] = mid_ref[...]
    gout[:, :, :, 0:CW] = gout[:, :, :, 0:CW] + cot_ref[...].astype(f32)
    for source, column, at in ((w_ref, 0, 0), (e_ref, 1, 29)):
        matrix = side_matrix(links_ref, column)
        for start in starts(24):
            got = dot(matrix, source[start : start + 16].reshape(256, CP)).reshape(16, SUB, CP)
            for n in range(16):
                if start == 8 and n < 8:
                    continue
                r, j = divmod(start + n, 3)
                gout[r, at + j] += got[n]
    def visit(r, carry):
        for h in range(2):
            low = gout[r, 16 * h : 16 * h + 16].astype(bf16).reshape(256, CP)
            low = dot(swap, low).astype(bf16)
            grad = dot(low, stem_t_ref[...]).astype(bf16)
            for s in range(SUB):
                out_ref[s & 3, (s >> 2) * QROWS + r, 16 * h : 16 * h + 16, :] = grad[
                    16 * s : 16 * s + 16
                ]
        return carry

    lax.fori_loop(0, QROWS, visit, 0)


def shifted(block, distance):
    count = lax.axis_size("tiles")
    return lax.ppermute(block, "tiles", [((i - distance) % count, i) for i in range(count)])


def levels():
    left, stride, out = lax.axis_size("tiles"), 1, []
    while left > 1:
        size = 2 if stride == 1 or left % 4 else 4
        out.append((stride, size))
        stride, left = stride * size, left // size
    return out


def rotated(block, level, distance):
    stride, size = level
    route = []
    for i in range(lax.axis_size("tiles")):
        place = (i // stride) % size
        route.append((i, i + ((place + distance) % size - place) * stride))
    return lax.ppermute(block, "tiles", route)


def place_in(level):
    stride, size = level
    return (lax.axis_index("tiles") // stride) % size


def tree_sum(terms):
    while len(terms) > 1:
        half = len(terms) // 2
        terms = [terms[n] + terms[n + half] for n in range(half)]
    return terms[0]


def scatter_sum(block, level):
    size = level[1]
    rows = block.shape[0] // size
    me = place_in(level)

    def piece(distance):
        return lax.dynamic_slice_in_dim(block, ((me + distance) % size) * rows, rows, 0)

    terms = [piece(0)] + [rotated(piece(n), level, n) for n in range(1, size)]
    return tree_sum([t.astype(f32) for t in terms]).astype(bf16)


def full_sum(block, level):
    terms = [block] + [rotated(block, level, n) for n in range(1, level[1])]
    return tree_sum([t.astype(f32) for t in terms])


def sum_and_gather(block, count, level):
    size = level[1]
    rows = block.shape[0] - count
    me = place_in(level)
    terms = [block] + [rotated(block, level, n) for n in range(1, size)]
    total = tree_sum([t[:count].astype(f32) for t in terms]).astype(bf16)
    out = jnp.zeros((rows * size,) + block.shape[1:], block.dtype)
    for n, term in enumerate(terms):
        out = lax.dynamic_update_slice_in_dim(out, term[count:], ((me - n) % size) * rows, 0)
    return jnp.concatenate([total, out], axis=0)


def body(
    ocean_state,
    cotangent,
    w_stem,
    dw_kernel,
    norm_gain,
    w_up,
    w_down,
    tile_links,
    fold_flags,
    wet_count,
):
    cin = ocean_state.shape[3]
    half_way = lax.axis_size("tiles") // 2
    pad = CP - CW
    stem_w = jnp.pad(w_stem, ((0, 0), (0, pad)))
    kb = jnp.pad(dw_kernel.reshape(49, 1, CW), ((0, 0), (0, 0), (0, pad)))
    kf = jnp.broadcast_to(kb.astype(f32), (49, 8, CP))
    diag = kb[:, :, :128] * jnp.eye(128, dtype=bf16)
    gain = jnp.pad(norm_gain, (0, pad))[None]
    up = jnp.pad(w_up, ((0, pad), (0, 0)))
    down_t = w_down.T

    strip = struct((QROWS, 3, SUB, cin), bf16)
    stem, moved, first, last = call(
        stem_kernel,
        [
            struct((QROWS, SIDE, SUB, CP), bf16),
            struct((QROWS, SIDE, SUB, cin), bf16),
            strip,
            strip,
        ],
        [VMEM, VMEM],
        micros=5,
    )(ocean_state, stem_w)
    from_west = shifted(last, 1).reshape(24, SUB, cin)
    from_east = shifted(first, -1).reshape(24, SUB, cin)
    cot = call(cot_kernel, struct((QROWS, SIDE, SUB, CW), bf16), [VMEM, SMEM], micros=5)(
        cotangent, wet_count
    )
    west_state, east_state, west, east, fold = call(
        widen_kernel,
        [struct((24, SUB, cin), bf16)] * 2
        + [struct((24, SUB, CP), bf16)] * 2
        + [struct((128, CP), bf16)],
        [VMEM] * 4 + [SMEM, SMEM],
        [pltpu.VMEM((128, CP), f32)],
    )(from_west, from_east, stem, stem_w, tile_links, fold_flags)
    partner = shifted(fold, half_way)
    ext0, ext1, gm0, gm1, gup, gdown, ggain, back = call(
        front_kernel,
        [
            struct((14 * EP, SUB, CP), bf16),
            struct((14 * EW, SUB, 128), bf16),
            struct((QROWS * GP, SUB, CP), bf16),
            struct((QROWS * GW, SUB, 128), bf16),
            struct((CP, FF), f32),
            struct((CW, FF), f32),
            struct((8, CP), f32),
            struct((128, CP), bf16),
        ],
        [VMEM] * 11 + [SMEM, SMEM],
        [
            pltpu.VMEM((QROWS, 16, 2, SUB, CP), f32),
            pltpu.VMEM((QROWS * GS, CP), f32),
            pltpu.VMEM((128, CP), f32),
        ],
        micros=36,
    )(stem, west, east, partner, cot, diag, kf, gain, up, up.T, down_t, tile_links, fold_flags)
    parts = [g[:CW, 256 * c : 256 * c + 256] for g in (gup, gdown) for c in range(3)]
    big = jnp.concatenate(parts, axis=0).astype(bf16)
    plan = levels()
    for level in plan[:3]:
        big = scatter_sum(big, level)
    partner_back = shifted(back, half_way)
    gkernel = call(
        taps_kernel,
        struct((49, CP), f32),
        [VMEM] * 4,
        [pltpu.VMEM((49, 8, CP), f32), pltpu.VMEM((CP, QROWS * 256), bf16)],
        micros=15,
    )(ext0, ext1, gm0, gm1)
    mid, back_w, back_e, gstem = call(
        back_kernel,
        [
            struct((QROWS, SIDE, SUB, CP), f32),
            struct((24, SUB, CP), bf16),
            struct((24, SUB, CP), bf16),
            struct((cin, CP), f32),
        ],
        [VMEM] * 9 + [SMEM, SMEM, pl.BlockSpec(memory_space=pl.ANY)],
        [
            pltpu.VMEM((14 * GP, SUB, CP), bf16),
            pltpu.VMEM((14 * GW, SUB, 128), bf16),
            pltpu.VMEM((QROWS, EP, 2, SUB, CP), f32),
        ],
        micros=20,
    )(
        gm0,
        gm1,
        diag,
        kf,
        partner_back,
        cot,
        moved,
        west_state,
        east_state,
        tile_links,
        fold_flags,
        gkernel,
    )
    back_from_west = shifted(back_e, 1)
    back_from_east = shifted(back_w, -1)
    grad_state = call(
        final_kernel,
        struct(ocean_state.shape, bf16),
        [VMEM] * 5 + [SMEM],
        [pltpu.VMEM((QROWS, SIDE, SUB, CP), f32)],
        micros=8,
    )(mid, cot, back_from_west, back_from_east, stem_w.T, tile_links)
    rest = jnp.concatenate(
        [gstem, gkernel, jnp.sum(ggain, axis=0, keepdims=True), jnp.zeros((15, CP), f32)], axis=0
    )
    count = rest.shape[0]
    pack = jnp.concatenate([rest.astype(bf16), big], axis=0)
    for level in plan[:2:-1]:
        pack = full_sum(pack, level).astype(bf16)
    for level in plan[2::-1]:
        pack = sum_and_gather(pack, count, level)
    rest = pack[:count].astype(f32)
    big = pack[count:].astype(f32).reshape(2, 3, CW, CP)
    gup = jnp.concatenate([big[0, c] for c in range(3)], axis=1)
    gdown = jnp.concatenate([big[1, c].T for c in range(3)], axis=0)
    gstem, gkernel, ggain = rest[:cin, :CW], rest[cin : cin + 49, :CW], rest[cin + 49, :CW]
    return (grad_state, gstem, gkernel.reshape(7, 7, CW), ggain, gup, gdown)


def solution(mesh):
    return jax.shard_map(
        body,
        mesh=mesh,
        in_specs=(
            P("tiles", None, None, None),
            P("tiles", None, None, None),
            P(),
            P(),
            P(),
            P(),
            P(),
            P("tiles", None),
            P("tiles"),
            P("tiles"),
        ),
        out_specs=(P("tiles", None, None, None), P(), P(), P(), P(), P()),
        check_vma=False,
    )
```

```python
import jax
import jax.numpy as jnp
from jax import lax
from jax.experimental import pallas as pl
from jax.experimental.pallas import tpu as pltpu
from jax.sharding import PartitionSpec as P


epsilon = 1e-06
root_half = 0.7071067811865476
inv_root_two_pi = 0.3989422804014327
SLOTS = 4
SIDE = 32
QROWS = 8
SUB = 16
CW = 192
CP = 256
FF = 768
EW = SIDE + 6
GW = SIDE + 12
EP = EW // 2
GP = GW // 2
GS = SIDE + 16
NFOLD = 3 * EW
bf16 = jnp.bfloat16
f32 = jnp.float32
VMEM = pl.BlockSpec(memory_space=pltpu.VMEM)
SMEM = pl.BlockSpec(memory_space=pltpu.SMEM)


def call(kernel, outs, specs, scratch=(), micros=1):
    single = not isinstance(outs, (list, tuple))
    return pl.pallas_call(
        kernel,
        out_shape=outs,
        in_specs=specs,
        out_specs=VMEM if single else [VMEM] * len(outs),
        scratch_shapes=list(scratch),
        compiler_params=pltpu.CompilerParams(vmem_limit_bytes=52 * 1024 * 1024),
        cost_estimate=pl.CostEstimate(
            flops=micros * 1_150_000_000, bytes_accessed=micros * 1_000_000, transcendentals=0
        ),
    )


def struct(shape, dtype):
    return jax.ShapeDtypeStruct(shape, dtype)


def dot(a, b):
    return jnp.dot(a, b, preferred_element_type=f32)


def dot_t(a, b):
    return lax.dot_general(a, b, (((0,), (0,)), ((), ())), preferred_element_type=f32)


def iotas():
    row = lax.broadcasted_iota(jnp.int32, (256, 256), 0)
    col = lax.broadcasted_iota(jnp.int32, (256, 256), 1)
    return row, col


def one_hot(mask):
    return jnp.where(mask, 1.0, 0.0).astype(bf16)


def swap_matrix():
    row, col = iotas()
    return one_hot(col == (row & 15) * 16 + (row >> 4))


def by_slot(slot, links_ref, column):
    link = jnp.full_like(slot, -1)
    for n in range(SLOTS):
        link = jnp.where(slot == n, links_ref[n, column], link)
    return link


def side_matrix(links_ref, column):
    row, col = iotas()
    s = row & 15
    link = by_slot(s & 3, links_ref, column)
    target = jnp.where(link >= 0, row - (s & 3) + link, -1)
    return one_hot(col == target)


def south_matrix(links_ref):
    row, col = iotas()
    s = row & 15
    link = by_slot(s & 3, links_ref, 2)
    target = jnp.where(s >= 4, row - 4, jnp.where(link >= 0, row - s + 12 + link, -1))
    return one_hot(col == target)


def north_matrix(links_ref):
    row, col = iotas()
    s = row & 15
    link = by_slot(s & 3, links_ref, 3)
    target = jnp.where(s < 12, row + 4, jnp.where(link >= 0, row - s + link, -1))
    return one_hot(col == target)


def starts(count):
    return [min(16 * n, count - 16) for n in range(-(-count // 16))]


def picked(matrix, block):
    lanes = block.shape[-1]
    return dot(matrix, block.reshape(256, lanes)).astype(bf16).reshape(16, SUB, lanes)


def fold_mask(flags_ref, shape):
    s = lax.broadcasted_iota(jnp.int32, shape, len(shape) - 2)
    mask = jnp.zeros(shape, jnp.int32)
    for n in range(SLOTS):
        mask = jnp.where(s == 12 + n, flags_ref[n], mask)
    return mask == 1


def fold_spread(flags_ref, start, step=1, parity=0):
    row = lax.broadcasted_iota(jnp.int32, (256, 128), 0)
    col = lax.broadcasted_iota(jnp.int32, (256, 128), 1)
    s = row & 15
    flag = jnp.zeros_like(s)
    for n in range(SLOTS):
        flag = jnp.where(s == 12 + n, flags_ref[n], flag)
    return one_hot((flag == 1) & (col == NFOLD - 1 - parity - step * (start + (row >> 4))))


def tap_of(a, b, flip):
    return (6 - a) * 7 + 6 - b if flip else a * 7 + b


def pair_weights(diag_ref, a, flip):
    def block(b):
        if 0 <= b <= 6:
            return diag_ref[tap_of(a, b, flip)]
        return jnp.zeros((128, 128), bf16)

    rows = [jnp.concatenate([block(m), block(m - 1)], axis=1) for m in range(8)]
    return jnp.concatenate(rows, axis=0)


def pair_term(src, bases, count, diag_ref, a, flip):
    parts = []
    for n in range(4):
        at = [src[pl.ds(base + n, count)].reshape(count * SUB, CP) for base in bases]
        parts.append(jnp.concatenate(at, axis=0))
    return dot(jnp.concatenate(parts, axis=1), pair_weights(diag_ref, a, flip))


def conv_pairs(src, base, width, count, diag_ref, flip):
    total = None
    for a in range(7):
        term = pair_term(src, [base + a * width], count, diag_ref, a, flip)
        total = term if total is None else total + term
    return total


def conv_rest(src, base, width, count, kf_ref, flip):
    total = jnp.zeros((count, 2, 8, 128), f32)
    for a in range(7):
        x = src[pl.ds(base + a * width, count + 6)].astype(f32).reshape(count + 6, 2, 8, 128)
        for b in range(7):
            total = total + x[b : b + count] * kf_ref[tap_of(a, b, flip), :, 128:]
    return total.reshape(count, SUB, 128)


def gelu_parts(hidden):
    cdf = 0.5 + 0.5 * lax.erf(hidden * root_half)
    bell = jnp.exp(-0.5 * hidden * hidden) * inv_root_two_pi
    return cdf, cdf + hidden * bell


def stem_kernel(state_ref, w_ref, stem_ref, moved_ref, first_ref, last_ref):
    swap = swap_matrix()
    w = w_ref[...]

    def visit(r, carry):
        for h in range(2):
            slabs = [
                state_ref[s & 3, (s >> 2) * QROWS + r, 16 * h : 16 * h + 16, :] for s in range(SUB)
            ]
            x = dot(swap, jnp.concatenate(slabs, axis=0)).astype(bf16)
            stem_ref[r, 16 * h : 16 * h + 16] = dot(x, w).astype(bf16).reshape(16, SUB, CP)
            x = x.reshape(16, SUB, -1)
            moved_ref[r, 16 * h : 16 * h + 16] = x
            if h == 0:
                first_ref[r] = x[:3]
            else:
                last_ref[r] = x[13:]
        return carry

    lax.fori_loop(0, QROWS, visit, 0, unroll=QROWS)


def cot_kernel(cot_ref, wet_ref, out_ref):
    swap = swap_matrix()

    def visit(r, carry):
        for h in range(2):
            slabs = []
            for s in range(SUB):
                slab = cot_ref[s & 3, (s >> 2) * QROWS + r, 16 * h : 16 * h + 16, :]
                slabs.append(jnp.where((s & 3) < wet_ref[0], slab, jnp.zeros_like(slab)))
            x = jnp.concatenate(slabs, axis=0)
            out_ref[r, 16 * h : 16 * h + 16] = dot(swap, x).astype(bf16).reshape(16, SUB, CW)
        return carry

    lax.fori_loop(0, QROWS, visit, 0, unroll=QROWS)


def widen_kernel(
    west_ref,
    east_ref,
    stem_ref,
    stem_w_ref,
    links_ref,
    flags_ref,
    ws_out,
    es_out,
    w_out,
    e_out,
    fold_out,
    rows,
):
    for source, column, raw, out in (
        (west_ref, 0, ws_out, w_out),
        (east_ref, 1, es_out, e_out),
    ):
        matrix = side_matrix(links_ref, column)
        for start in starts(24):
            got = picked(matrix, source[start : start + 16])
            raw[start : start + 16] = got
            got = dot(got.reshape(256, -1), stem_w_ref[...]).astype(bf16)
            out[start : start + 16] = got.reshape(16, SUB, CP)
    mask = fold_mask(flags_ref, (1, SUB, CP))
    rows[...] = jnp.zeros_like(rows)

    def chosen(block):
        return jnp.sum(jnp.where(mask, block.astype(f32), 0.0), axis=1)

    for k in range(3):
        rows[k * EW : k * EW + 3] = chosen(w_out[(5 + k) * 3 : (6 + k) * 3])
        rows[k * EW + 3 : k * EW + 35] = chosen(stem_ref[5 + k])
        rows[k * EW + 35 : k * EW + 38] = chosen(e_out[(5 + k) * 3 : (6 + k) * 3])
    fold_out[...] = rows[...].astype(bf16)


def fill_halo(ref, width, links_ref):
    south = south_matrix(links_ref)
    north = north_matrix(links_ref)
    for start in starts(3 * width):
        ref[start : start + 16] = picked(south, ref[8 * width + start : 8 * width + start + 16])
        top = 11 * width + start
        ref[top : top + 16] = picked(north, ref[3 * width + start : 3 * width + start + 16])


def front_kernel(
    stem_ref,
    w_ref,
    e_ref,
    partner_ref,
    cot_ref,
    diag_ref,
    kf_ref,
    gain_ref,
    up_ref,
    up_t_ref,
    down_t_ref,
    links_ref,
    flags_ref,
    ext0_ref,
    ext1_ref,
    gm0_ref,
    gm1_ref,
    gup_ref,
    gdown_ref,
    ggain_ref,
    back_ref,
    mixed_ref,
    chosen_ref,
    rows_ref,
):
    for r in range(QROWS):
        west, east = w_ref[3 * r : 3 * r + 3], e_ref[3 * r : 3 * r + 3]
        x = jnp.concatenate([west, stem_ref[r], east], axis=0)
        pairs = x[:, :, :128].reshape(EP, 2, SUB, 128)
        ext0_ref[(r + 3) * EP : (r + 4) * EP, :, :128] = pairs[:, 0]
        ext0_ref[(r + 3) * EP : (r + 4) * EP, :, 128:] = pairs[:, 1]
        ext1_ref[(r + 3) * EW : (r + 4) * EW] = x[:, :, 128:]
    fill_halo(ext0_ref, EP, links_ref)
    fill_halo(ext1_ref, EW, links_ref)
    partner = partner_ref[...]
    mask = fold_mask(flags_ref, (1, SUB, CP))
    for start in starts(3 * EP):
        top = 11 * EP + start
        halves = [dot(fold_spread(flags_ref, start, 2, n), partner[:, :128]) for n in range(2)]
        add = jnp.concatenate(halves, axis=1).astype(bf16).reshape(16, SUB, CP)
        ext0_ref[top : top + 16] = jnp.where(mask, add, ext0_ref[top : top + 16])
    for start in starts(NFOLD):
        top = 11 * EW + start
        add = dot(fold_spread(flags_ref, start), partner[:, 128:]).astype(bf16)
        ext1_ref[top : top + 16] = jnp.where(
            mask[:, :, :128], add.reshape(16, SUB, 128), ext1_ref[top : top + 16]
        )
    gm0_ref[...] = jnp.zeros_like(gm0_ref)
    gm1_ref[...] = jnp.zeros_like(gm1_ref)
    gup_ref[...] = jnp.zeros_like(gup_ref)
    gdown_ref[...] = jnp.zeros_like(gdown_ref)
    ggain_ref[...] = jnp.zeros_like(ggain_ref)
    chosen_ref[...] = jnp.zeros_like(chosen_ref)

    def mix(r, carry):
        pairs = conv_pairs(ext0_ref, r * EP, EP, 16, diag_ref, False)
        for n in range(2):
            half = pairs[:, 128 * n : 128 * n + 128]
            mixed_ref[r, :, n, :, :128] = half.reshape(16, SUB, 128)
        for block in range(4):
            mixed_ref[r, 4 * block : 4 * block + 4, :, :, 128:] = conv_rest(
                ext1_ref, r * EW + 8 * block, EW, 8, kf_ref, False
            ).reshape(4, 2, SUB, 128)
        return carry

    lax.fori_loop(0, QROWS, mix, 0)

    def visit(r, carry):
        mixed = mixed_ref[r].reshape(512, CP)
        lane = lax.broadcasted_iota(jnp.int32, (1, CP), 1)
        average = jnp.sum(mixed, axis=-1, keepdims=True) * (1.0 / CW)
        centred = jnp.where(lane < CW, mixed - average, 0.0)
        variance = jnp.sum(centred * centred, axis=-1, keepdims=True) * (1.0 / CW)
        inv_std = lax.rsqrt(variance + epsilon)
        normed = centred * inv_std
        gain = gain_ref[...]
        low = (normed * gain).astype(bf16)
        cot = cot_ref[r].reshape(512, CW)
        grad_normed = jnp.zeros((512, CP), f32)
        for c in range(3):
            cols = slice(256 * c, 256 * c + 256)
            hidden = dot(low, up_ref[:, cols])
            grad_act = dot(cot, down_t_ref[:, cols])
            cdf, slope = gelu_parts(hidden)
            act = (hidden * cdf).astype(bf16)
            grad_hidden = (grad_act * slope).astype(bf16)
            gdown_ref[:, cols] += dot_t(cot, act)
            gup_ref[:, cols] += dot_t(low, grad_hidden)
            grad_normed = grad_normed + dot(grad_hidden, up_t_ref[cols, :])
        product = grad_normed * normed
        ggain_ref[...] += jnp.sum(product.reshape(64, 8, CP), axis=0)
        grad_unit = grad_normed * gain
        mean_unit = jnp.sum(grad_unit, axis=-1, keepdims=True) * (1.0 / CW)
        mean_both = jnp.sum(product * gain, axis=-1, keepdims=True) * (1.0 / CW)
        grad_mixed = inv_std * (grad_unit - mean_unit - normed * mean_both)
        slots = grad_mixed.reshape(SIDE, SUB, CP)
        chosen_ref[pl.ds(r * GS + 8, SIDE)] = jnp.sum(jnp.where(mask, slots, 0.0), axis=1)
        low_mixed = slots.astype(bf16)
        pairs = low_mixed[:, :, :128].reshape(16, 2, SUB, 128)
        gm0_ref[pl.ds(r * GP + 3, 16), :, :128] = pairs[:, 0]
        gm0_ref[pl.ds(r * GP + 3, 16), :, 128:] = pairs[:, 1]
        gm1_ref[pl.ds(r * GW + 6, SIDE)] = low_mixed[:, :, 128:]
        return carry

    lax.fori_loop(0, QROWS, visit, 0, unroll=2)
    rows_ref[...] = jnp.zeros_like(rows_ref)
    for t in range(3):
        total = jnp.zeros((EW, CP), f32)
        for a in range(4 + t, 7):
            x = chosen_ref[(11 + t - a) * GS : (12 + t - a) * GS]
            for b in range(7):
                total = total + x[8 - b : 8 - b + EW] * kf_ref[a * 7 + b, 0:1, :]
        rows_ref[t * EW : t * EW + EW] = total
    back_ref[...] = rows_ref[...].astype(bf16)


def taps_kernel(ext0_ref, ext1_ref, gm0_ref, gm1_ref, out_ref, acc_ref, turned_ref):
    acc_ref[...] = jnp.zeros_like(acc_ref)
    for r in range(QROWS):
        g = gm0_ref[r * GP + 3 : r * GP + 19].reshape(256, CP)
        turned_ref[:, 256 * r : 256 * r + 256] = g.T
    row = lax.broadcasted_iota(jnp.int32, (128, 128), 0)
    col = lax.broadcasted_iota(jnp.int32, (128, 128), 1)
    diagonal = row == col

    def visit(a, carry):
        turned = turned_ref[...]
        sums = [jnp.zeros((8, 128), f32) for _ in range(7)]
        for n in range(4):
            at = [ext0_ref[pl.ds((r + a) * EP + n, 16)].reshape(256, CP) for r in range(QROWS)]
            both = dot(turned, jnp.concatenate(at, axis=0))
            for out_col in range(2):
                for in_col in range(2):
                    b = 2 * n + in_col - out_col
                    if 0 <= b <= 6:
                        part = both[
                            128 * out_col : 128 * out_col + 128, 128 * in_col : 128 * in_col + 128
                        ]
                        part = jnp.where(diagonal, part, 0.0).reshape(16, 8, 128)
                        sums[b] = sums[b] + jnp.sum(part, axis=0)
        for b in range(7):
            acc_ref[a * 7 + b, :, :128] += sums[b]
        rest = [jnp.zeros((2, 8, 128), f32) for _ in range(7)]
        for r in range(QROWS):
            for block in range(4):
                x = ext1_ref[pl.ds((r + a) * EW + 8 * block, 14)].astype(f32)
                g = gm1_ref[r * GW + 6 + 8 * block : r * GW + 14 + 8 * block].astype(f32)
                x = x.reshape(14, 2, 8, 128)
                g = g.reshape(8, 2, 8, 128)
                for b in range(7):
                    for n in range(8):
                        rest[b] = rest[b] + x[b + n] * g[n]
        for b in range(7):
            acc_ref[a * 7 + b, :, 128:] += rest[b][0] + rest[b][1]
        return carry

    lax.fori_loop(0, 7, visit, 0)
    out_ref[...] = jnp.sum(acc_ref[...], axis=1)


def back_kernel(
    gm0_ref,
    gm1_ref,
    diag_ref,
    kf_ref,
    partner_ref,
    cot_ref,
    moved_ref,
    ws_ref,
    es_ref,
    links_ref,
    flags_ref,
    after_ref,
    mid_ref,
    w_ref,
    e_ref,
    gstem_ref,
    gmx0,
    gmx1,
    row,
):
    for source, target, width in ((gm0_ref, gmx0, GP), (gm1_ref, gmx1, GW)):
        edge = jnp.zeros((3 * width, SUB, target.shape[-1]), bf16)
        target[0 : 3 * width] = edge
        target[3 * width : 11 * width] = source[...]
        target[11 * width : 14 * width] = edge
        fill_halo(target, width, links_ref)

    def visit(r, carry):
        pairs = conv_pairs(gmx0, r * GP, GP, EP, diag_ref, True)
        for n in range(2):
            row[r, :, n, :, :128] = pairs[:, 128 * n : 128 * n + 128].reshape(EP, SUB, 128)
        for q in range(0, EW, 8):
            count = min(8, EW - q)
            row[r, q // 2 : (q + count) // 2, :, :, 128:] = conv_rest(
                gmx1, r * GW + q, GW, count, kf_ref, True
            ).reshape(count // 2, 2, SUB, 128)
        return carry

    lax.fori_loop(0, QROWS, visit, 0)
    partner = partner_ref[...]
    for k in range(3):
        for q in (0, 16, EW - 16):
            skip = 10 if q == EW - 16 else 0
            add = dot(fold_spread(flags_ref, k * EW + q), partner).reshape(16, SUB, CP)
            row[5 + k, (q + skip) // 2 : q // 2 + 8] += add[skip:].reshape(-1, 2, SUB, CP)
    for r in range(QROWS):
        full = row[r].reshape(EW, SUB, CP)
        mid_ref[r] = full[3:35]
        w_ref[3 * r : 3 * r + 3] = full[0:3].astype(bf16)
        e_ref[3 * r : 3 * r + 3] = full[35:38].astype(bf16)
    cin = moved_ref.shape[-1]
    gstem = dot_t(ws_ref[...].reshape(24 * SUB, cin), w_ref[...].reshape(24 * SUB, CP))
    gstem += dot_t(es_ref[...].reshape(24 * SUB, cin), e_ref[...].reshape(24 * SUB, CP))
    gstem_ref[...] = gstem
    for r in range(QROWS):
        own = mid_ref[r, :, :, :CW] + cot_ref[r].astype(f32)
        own = own.astype(bf16).reshape(SIDE * SUB, CW)
        gstem_ref[:, :CW] += dot_t(moved_ref[r].reshape(SIDE * SUB, cin), own)


def final_kernel(
    mid_ref, cot_ref, w_ref, e_ref, stem_t_ref, links_ref, out_ref, gout
):
    swap = swap_matrix()
    gout[...] = mid_ref[...]
    gout[:, :, :, 0:CW] = gout[:, :, :, 0:CW] + cot_ref[...].astype(f32)
    for source, column, at in ((w_ref, 0, 0), (e_ref, 1, 29)):
        matrix = side_matrix(links_ref, column)
        for start in starts(24):
            got = dot(matrix, source[start : start + 16].reshape(256, CP)).reshape(16, SUB, CP)
            for n in range(16):
                if start == 8 and n < 8:
                    continue
                r, j = divmod(start + n, 3)
                gout[r, at + j] += got[n]
    def visit(r, carry):
        for h in range(2):
            low = gout[r, 16 * h : 16 * h + 16].astype(bf16).reshape(256, CP)
            low = dot(swap, low).astype(bf16)
            grad = dot(low, stem_t_ref[...]).astype(bf16)
            for s in range(SUB):
                out_ref[s & 3, (s >> 2) * QROWS + r, 16 * h : 16 * h + 16, :] = grad[
                    16 * s : 16 * s + 16
                ]
        return carry

    lax.fori_loop(0, QROWS, visit, 0, unroll=QROWS)


def shifted(block, distance):
    count = lax.axis_size("tiles")
    return lax.ppermute(block, "tiles", [((i - distance) % count, i) for i in range(count)])


def levels():
    left, stride, out = lax.axis_size("tiles"), 1, []
    while left > 1:
        size = 2 if stride == 1 or left % 4 else 4
        out.append((stride, size))
        stride, left = stride * size, left // size
    return out


def rotated(block, level, distance):
    stride, size = level
    route = []
    for i in range(lax.axis_size("tiles")):
        place = (i // stride) % size
        route.append((i, i + ((place + distance) % size - place) * stride))
    return lax.ppermute(block, "tiles", route)


def place_in(level):
    stride, size = level
    return (lax.axis_index("tiles") // stride) % size


def tree_sum(terms):
    while len(terms) > 1:
        half = len(terms) // 2
        terms = [terms[n] + terms[n + half] for n in range(half)]
    return terms[0]


def scatter_sum(block, level):
    size = level[1]
    rows = block.shape[0] // size
    me = place_in(level)

    def piece(distance):
        return lax.dynamic_slice_in_dim(block, ((me + distance) % size) * rows, rows, 0)

    terms = [piece(0)] + [rotated(piece(n), level, n) for n in range(1, size)]
    return tree_sum([t.astype(f32) for t in terms]).astype(bf16)


def full_sum(block, level):
    terms = [block] + [rotated(block, level, n) for n in range(1, level[1])]
    return tree_sum([t.astype(f32) for t in terms])


def sum_kernel(*refs):
    *terms, after_ref, out_ref = refs
    rows = out_ref.shape[0]
    out_ref[...] = tree_sum([t[:rows].astype(f32) for t in terms]).astype(bf16)


def sum_and_gather(block, count, level, after):
    size = level[1]
    rows = block.shape[0] - count
    me = place_in(level)
    terms = [block] + [rotated(block, level, n) for n in range(1, size)]
    if after is None:
        total = tree_sum([t[:count].astype(f32) for t in terms]).astype(bf16)
    else:
        total = call(
            sum_kernel,
            struct((count, block.shape[1]), bf16),
            [VMEM] * size + [pl.BlockSpec(memory_space=pl.ANY)],
        )(*terms, after)
    out = jnp.zeros((rows * size,) + block.shape[1:], block.dtype)
    for n, term in enumerate(terms):
        out = lax.dynamic_update_slice_in_dim(out, term[count:], ((me - n) % size) * rows, 0)
    return jnp.concatenate([total, out], axis=0)


def body(
    ocean_state,
    cotangent,
    w_stem,
    dw_kernel,
    norm_gain,
    w_up,
    w_down,
    tile_links,
    fold_flags,
    wet_count,
):
    cin = ocean_state.shape[3]
    half_way = lax.axis_size("tiles") // 2
    pad = CP - CW
    stem_w = jnp.pad(w_stem, ((0, 0), (0, pad)))
    kb = jnp.pad(dw_kernel.reshape(49, 1, CW), ((0, 0), (0, 0), (0, pad)))
    kf = jnp.broadcast_to(kb.astype(f32), (49, 8, CP))
    diag = kb[:, :, :128] * jnp.eye(128, dtype=bf16)
    gain = jnp.pad(norm_gain, (0, pad))[None]
    up = jnp.pad(w_up, ((0, pad), (0, 0)))
    down_t = w_down.T

    strip = struct((QROWS, 3, SUB, cin), bf16)
    stem, moved, first, last = call(
        stem_kernel,
        [
            struct((QROWS, SIDE, SUB, CP), bf16),
            struct((QROWS, SIDE, SUB, cin), bf16),
            strip,
            strip,
        ],
        [VMEM, VMEM],
        micros=5,
    )(ocean_state, stem_w)
    from_west = shifted(last, 1).reshape(24, SUB, cin)
    from_east = shifted(first, -1).reshape(24, SUB, cin)
    cot = call(cot_kernel, struct((QROWS, SIDE, SUB, CW), bf16), [VMEM, SMEM], micros=5)(
        cotangent, wet_count
    )
    west_state, east_state, west, east, fold = call(
        widen_kernel,
        [struct((24, SUB, cin), bf16)] * 2
        + [struct((24, SUB, CP), bf16)] * 2
        + [struct((128, CP), bf16)],
        [VMEM] * 4 + [SMEM, SMEM],
        [pltpu.VMEM((128, CP), f32)],
    )(from_west, from_east, stem, stem_w, tile_links, fold_flags)
    partner = shifted(fold, half_way)
    ext0, ext1, gm0, gm1, gup, gdown, ggain, back = call(
        front_kernel,
        [
            struct((14 * EP, SUB, CP), bf16),
            struct((14 * EW, SUB, 128), bf16),
            struct((QROWS * GP, SUB, CP), bf16),
            struct((QROWS * GW, SUB, 128), bf16),
            struct((CP, FF), f32),
            struct((CW, FF), f32),
            struct((8, CP), f32),
            struct((128, CP), bf16),
        ],
        [VMEM] * 11 + [SMEM, SMEM],
        [
            pltpu.VMEM((QROWS, 16, 2, SUB, CP), f32),
            pltpu.VMEM((QROWS * GS, CP), f32),
            pltpu.VMEM((128, CP), f32),
        ],
        micros=36,
    )(stem, west, east, partner, cot, diag, kf, gain, up, up.T, down_t, tile_links, fold_flags)
    parts = [g[:CW, 256 * c : 256 * c + 256] for g in (gup, gdown) for c in range(3)]
    big = jnp.concatenate(parts, axis=0).astype(bf16)
    plan = levels()
    for level in plan[:3]:
        big = scatter_sum(big, level)
    partner_back = shifted(back, half_way)
    gkernel = call(
        taps_kernel,
        struct((49, CP), f32),
        [VMEM] * 4,
        [pltpu.VMEM((49, 8, CP), f32), pltpu.VMEM((CP, QROWS * 256), bf16)],
        micros=15,
    )(ext0, ext1, gm0, gm1)
    mid, back_w, back_e, gstem = call(
        back_kernel,
        [
            struct((QROWS, SIDE, SUB, CP), f32),
            struct((24, SUB, CP), bf16),
            struct((24, SUB, CP), bf16),
            struct((cin, CP), f32),
        ],
        [VMEM] * 9 + [SMEM, SMEM, pl.BlockSpec(memory_space=pl.ANY)],
        [
            pltpu.VMEM((14 * GP, SUB, CP), bf16),
            pltpu.VMEM((14 * GW, SUB, 128), bf16),
            pltpu.VMEM((QROWS, EP, 2, SUB, CP), f32),
        ],
        micros=20,
    )(
        gm0,
        gm1,
        diag,
        kf,
        partner_back,
        cot,
        moved,
        west_state,
        east_state,
        tile_links,
        fold_flags,
        gkernel,
    )
    back_from_west = shifted(back_e, 1)
    back_from_east = shifted(back_w, -1)
    grad_state = call(
        final_kernel,
        struct(ocean_state.shape, bf16),
        [VMEM] * 5 + [SMEM],
        [pltpu.VMEM((QROWS, SIDE, SUB, CP), f32)],
        micros=8,
    )(mid, cot, back_from_west, back_from_east, stem_w.T, tile_links)
    rest = jnp.concatenate(
        [gstem, gkernel, jnp.sum(ggain, axis=0, keepdims=True), jnp.zeros((15, CP), f32)], axis=0
    )
    count = rest.shape[0]
    pack = jnp.concatenate([rest.astype(bf16), big], axis=0)
    for level in plan[:2:-1]:
        pack = full_sum(pack, level).astype(bf16)
    for level in plan[2::-1]:
        after = grad_state if level == plan[:3][-1] else None
        pack = sum_and_gather(pack, count, level, after)
    rest = pack[:count].astype(f32)
    big = pack[count:].astype(f32).reshape(2, 3, CW, CP)
    gup = jnp.concatenate([big[0, c] for c in range(3)], axis=1)
    gdown = jnp.concatenate([big[1, c].T for c in range(3)], axis=0)
    gstem, gkernel, ggain = rest[:cin, :CW], rest[cin : cin + 49, :CW], rest[cin + 49, :CW]
    return (grad_state, gstem, gkernel.reshape(7, 7, CW), ggain, gup, gdown)


def solution(mesh):
    return jax.shard_map(
        body,
        mesh=mesh,
        in_specs=(
            P("tiles", None, None, None),
            P("tiles", None, None, None),
            P(),
            P(),
            P(),
            P(),
            P(),
            P("tiles", None),
            P("tiles"),
            P("tiles"),
        ),
        out_specs=(P("tiles", None, None, None), P(), P(), P(), P(), P()),
        check_vma=False,
    )
```

```python
import jax
import jax.numpy as jnp
from jax import lax
from jax.experimental import pallas as pl
from jax.experimental.pallas import tpu as pltpu
from jax.sharding import PartitionSpec as P


epsilon = 1e-06
root_half = 0.7071067811865476
inv_root_two_pi = 0.3989422804014327
SLOTS = 4
SIDE = 32
QROWS = 8
SUB = 16
CW = 192
CP = 256
FF = 768
EW = SIDE + 6
GW = SIDE + 12
EP = EW // 2
GP = GW // 2
GS = SIDE + 16
NFOLD = 3 * EW
bf16 = jnp.bfloat16
f32 = jnp.float32
VMEM = pl.BlockSpec(memory_space=pltpu.VMEM)
SMEM = pl.BlockSpec(memory_space=pltpu.SMEM)


def call(kernel, outs, specs, scratch=(), micros=1):
    single = not isinstance(outs, (list, tuple))
    return pl.pallas_call(
        kernel,
        out_shape=outs,
        in_specs=specs,
        out_specs=VMEM if single else [VMEM] * len(outs),
        scratch_shapes=list(scratch),
        compiler_params=pltpu.CompilerParams(vmem_limit_bytes=52 * 1024 * 1024),
        cost_estimate=pl.CostEstimate(
            flops=micros * 1_150_000_000, bytes_accessed=micros * 1_000_000, transcendentals=0
        ),
    )


def struct(shape, dtype):
    return jax.ShapeDtypeStruct(shape, dtype)


def dot(a, b):
    return jnp.dot(a, b, preferred_element_type=f32)


def dot_t(a, b):
    return lax.dot_general(a, b, (((0,), (0,)), ((), ())), preferred_element_type=f32)


def iotas():
    row = lax.broadcasted_iota(jnp.int32, (256, 256), 0)
    col = lax.broadcasted_iota(jnp.int32, (256, 256), 1)
    return row, col


def one_hot(mask):
    return jnp.where(mask, 1.0, 0.0).astype(bf16)


def swap_matrix():
    row, col = iotas()
    return one_hot(col == (row & 15) * 16 + (row >> 4))


def by_slot(slot, links_ref, column):
    link = jnp.full_like(slot, -1)
    for n in range(SLOTS):
        link = jnp.where(slot == n, links_ref[n, column], link)
    return link


def side_matrix(links_ref, column):
    row, col = iotas()
    s = row & 15
    link = by_slot(s & 3, links_ref, column)
    target = jnp.where(link >= 0, row - (s & 3) + link, -1)
    return one_hot(col == target)


def south_matrix(links_ref):
    row, col = iotas()
    s = row & 15
    link = by_slot(s & 3, links_ref, 2)
    target = jnp.where(s >= 4, row - 4, jnp.where(link >= 0, row - s + 12 + link, -1))
    return one_hot(col == target)


def north_matrix(links_ref):
    row, col = iotas()
    s = row & 15
    link = by_slot(s & 3, links_ref, 3)
    target = jnp.where(s < 12, row + 4, jnp.where(link >= 0, row - s + link, -1))
    return one_hot(col == target)


def starts(count):
    return [min(16 * n, count - 16) for n in range(-(-count // 16))]


def picked(matrix, block):
    lanes = block.shape[-1]
    return dot(matrix, block.reshape(256, lanes)).astype(bf16).reshape(16, SUB, lanes)


def fold_mask(flags_ref, shape):
    s = lax.broadcasted_iota(jnp.int32, shape, len(shape) - 2)
    mask = jnp.zeros(shape, jnp.int32)
    for n in range(SLOTS):
        mask = jnp.where(s == 12 + n, flags_ref[n], mask)
    return mask == 1


def fold_spread(flags_ref, start, step=1, parity=0):
    row = lax.broadcasted_iota(jnp.int32, (256, 128), 0)
    col = lax.broadcasted_iota(jnp.int32, (256, 128), 1)
    s = row & 15
    flag = jnp.zeros_like(s)
    for n in range(SLOTS):
        flag = jnp.where(s == 12 + n, flags_ref[n], flag)
    return one_hot((flag == 1) & (col == NFOLD - 1 - parity - step * (start + (row >> 4))))


def tap_of(a, b, flip):
    return (6 - a) * 7 + 6 - b if flip else a * 7 + b


def pair_weights(diag_ref, a, flip):
    def block(b):
        if 0 <= b <= 6:
            return diag_ref[tap_of(a, b, flip)]
        return jnp.zeros((128, 128), bf16)

    rows = [jnp.concatenate([block(m), block(m - 1)], axis=1) for m in range(8)]
    return jnp.concatenate(rows, axis=0)


def pair_term(src, bases, count, diag_ref, a, flip):
    parts = []
    for n in range(4):
        at = [src[pl.ds(base + n, count)].reshape(count * SUB, CP) for base in bases]
        parts.append(jnp.concatenate(at, axis=0))
    return dot(jnp.concatenate(parts, axis=1), pair_weights(diag_ref, a, flip))


def conv_pairs(src, base, width, count, diag_ref, flip):
    total = None
    for a in range(7):
        term = pair_term(src, [base + a * width], count, diag_ref, a, flip)
        total = term if total is None else total + term
    return total


def conv_rest(src, base, width, count, kf_ref, flip):
    total = jnp.zeros((count, 2, 8, 128), f32)
    for a in range(7):
        x = src[pl.ds(base + a * width, count + 6)].astype(f32).reshape(count + 6, 2, 8, 128)
        for b in range(7):
            total = total + x[b : b + count] * kf_ref[tap_of(a, b, flip), :, 128:]
    return total.reshape(count, SUB, 128)


def gelu_parts(hidden):
    cdf = 0.5 + 0.5 * lax.erf(hidden * root_half)
    bell = jnp.exp(-0.5 * hidden * hidden) * inv_root_two_pi
    return cdf, cdf + hidden * bell


def stem_kernel(state_ref, w_ref, stem_ref, moved_ref, first_ref, last_ref):
    swap = swap_matrix()
    w = w_ref[...]

    def visit(r, carry):
        for h in range(2):
            slabs = [
                state_ref[s & 3, (s >> 2) * QROWS + r, 16 * h : 16 * h + 16, :] for s in range(SUB)
            ]
            x = dot(swap, jnp.concatenate(slabs, axis=0)).astype(bf16)
            stem_ref[r, 16 * h : 16 * h + 16] = dot(x, w).astype(bf16).reshape(16, SUB, CP)
            x = x.reshape(16, SUB, -1)
            moved_ref[r, 16 * h : 16 * h + 16] = x
            if h == 0:
                first_ref[r] = x[:3]
            else:
                last_ref[r] = x[13:]
        return carry

    lax.fori_loop(0, QROWS, visit, 0, unroll=QROWS)


def cot_kernel(cot_ref, wet_ref, out_ref):
    swap = swap_matrix()

    def visit(r, carry):
        for h in range(2):
            slabs = []
            for s in range(SUB):
                slab = cot_ref[s & 3, (s >> 2) * QROWS + r, 16 * h : 16 * h + 16, :]
                slabs.append(jnp.where((s & 3) < wet_ref[0], slab, jnp.zeros_like(slab)))
            x = jnp.concatenate(slabs, axis=0)
            out_ref[r, 16 * h : 16 * h + 16] = dot(swap, x).astype(bf16).reshape(16, SUB, CW)
        return carry

    lax.fori_loop(0, QROWS, visit, 0, unroll=QROWS)


def widen_kernel(
    west_ref,
    east_ref,
    stem_ref,
    stem_w_ref,
    links_ref,
    flags_ref,
    ws_out,
    es_out,
    w_out,
    e_out,
    fold_out,
    rows,
):
    for source, column, raw, out in (
        (west_ref, 0, ws_out, w_out),
        (east_ref, 1, es_out, e_out),
    ):
        matrix = side_matrix(links_ref, column)
        for start in starts(24):
            got = picked(matrix, source[start : start + 16])
            raw[start : start + 16] = got
            got = dot(got.reshape(256, -1), stem_w_ref[...]).astype(bf16)
            out[start : start + 16] = got.reshape(16, SUB, CP)
    mask = fold_mask(flags_ref, (1, SUB, CP))
    rows[...] = jnp.zeros_like(rows)

    def chosen(block):
        return jnp.sum(jnp.where(mask, block.astype(f32), 0.0), axis=1)

    for k in range(3):
        rows[k * EW : k * EW + 3] = chosen(w_out[(5 + k) * 3 : (6 + k) * 3])
        rows[k * EW + 3 : k * EW + 35] = chosen(stem_ref[5 + k])
        rows[k * EW + 35 : k * EW + 38] = chosen(e_out[(5 + k) * 3 : (6 + k) * 3])
    fold_out[...] = rows[...].astype(bf16)


def fill_halo(ref, width, links_ref):
    south = south_matrix(links_ref)
    north = north_matrix(links_ref)
    for start in starts(3 * width):
        ref[start : start + 16] = picked(south, ref[8 * width + start : 8 * width + start + 16])
        top = 11 * width + start
        ref[top : top + 16] = picked(north, ref[3 * width + start : 3 * width + start + 16])


def front_kernel(
    stem_ref,
    w_ref,
    e_ref,
    partner_ref,
    cot_ref,
    diag_ref,
    kf_ref,
    gain_ref,
    up_ref,
    up_t_ref,
    down_t_ref,
    links_ref,
    flags_ref,
    ext0_ref,
    ext1_ref,
    gm0_ref,
    gm1_ref,
    big_ref,
    ggain_ref,
    back_ref,
    mixed_ref,
    chosen_ref,
    rows_ref,
    gup_ref,
    gdown_ref,
):
    for r in range(QROWS):
        west, east = w_ref[3 * r : 3 * r + 3], e_ref[3 * r : 3 * r + 3]
        x = jnp.concatenate([west, stem_ref[r], east], axis=0)
        pairs = x[:, :, :128].reshape(EP, 2, SUB, 128)
        ext0_ref[(r + 3) * EP : (r + 4) * EP, :, :128] = pairs[:, 0]
        ext0_ref[(r + 3) * EP : (r + 4) * EP, :, 128:] = pairs[:, 1]
        ext1_ref[(r + 3) * EW : (r + 4) * EW] = x[:, :, 128:]
    fill_halo(ext0_ref, EP, links_ref)
    fill_halo(ext1_ref, EW, links_ref)
    partner = partner_ref[...]
    mask = fold_mask(flags_ref, (1, SUB, CP))
    for start in starts(3 * EP):
        top = 11 * EP + start
        halves = [dot(fold_spread(flags_ref, start, 2, n), partner[:, :128]) for n in range(2)]
        add = jnp.concatenate(halves, axis=1).astype(bf16).reshape(16, SUB, CP)
        ext0_ref[top : top + 16] = jnp.where(mask, add, ext0_ref[top : top + 16])
    for start in starts(NFOLD):
        top = 11 * EW + start
        add = dot(fold_spread(flags_ref, start), partner[:, 128:]).astype(bf16)
        ext1_ref[top : top + 16] = jnp.where(
            mask[:, :, :128], add.reshape(16, SUB, 128), ext1_ref[top : top + 16]
        )
    gm0_ref[...] = jnp.zeros_like(gm0_ref)
    gm1_ref[...] = jnp.zeros_like(gm1_ref)
    gup_ref[...] = jnp.zeros_like(gup_ref)
    gdown_ref[...] = jnp.zeros_like(gdown_ref)
    ggain_ref[...] = jnp.zeros_like(ggain_ref)
    chosen_ref[...] = jnp.zeros_like(chosen_ref)

    def mix(r, carry):
        pairs = conv_pairs(ext0_ref, r * EP, EP, 16, diag_ref, False)
        for n in range(2):
            half = pairs[:, 128 * n : 128 * n + 128]
            mixed_ref[r, :, n, :, :128] = half.reshape(16, SUB, 128)
        for block in range(4):
            mixed_ref[r, 4 * block : 4 * block + 4, :, :, 128:] = conv_rest(
                ext1_ref, r * EW + 8 * block, EW, 8, kf_ref, False
            ).reshape(4, 2, SUB, 128)
        return carry

    lax.fori_loop(0, QROWS, mix, 0)

    def visit(r, carry):
        mixed = mixed_ref[r].reshape(512, CP)
        lane = lax.broadcasted_iota(jnp.int32, (1, CP), 1)
        average = jnp.sum(mixed, axis=-1, keepdims=True) * (1.0 / CW)
        centred = jnp.where(lane < CW, mixed - average, 0.0)
        variance = jnp.sum(centred * centred, axis=-1, keepdims=True) * (1.0 / CW)
        inv_std = lax.rsqrt(variance + epsilon)
        normed = centred * inv_std
        gain = gain_ref[...]
        low = (normed * gain).astype(bf16)
        cot = cot_ref[r].reshape(512, CW)
        grad_normed = jnp.zeros((512, CP), f32)
        for c in range(3):
            cols = slice(256 * c, 256 * c + 256)
            hidden = dot(low, up_ref[:, cols])
            grad_act = dot(cot, down_t_ref[:, cols])
            cdf, slope = gelu_parts(hidden)
            act = (hidden * cdf).astype(bf16)
            grad_hidden = (grad_act * slope).astype(bf16)
            gdown_ref[:, cols] += dot_t(cot, act)
            gup_ref[:, cols] += dot_t(low, grad_hidden)
            grad_normed = grad_normed + dot(grad_hidden, up_t_ref[cols, :])
        product = grad_normed * normed
        ggain_ref[...] += jnp.sum(product.reshape(64, 8, CP), axis=0)
        grad_unit = grad_normed * gain
        mean_unit = jnp.sum(grad_unit, axis=-1, keepdims=True) * (1.0 / CW)
        mean_both = jnp.sum(product * gain, axis=-1, keepdims=True) * (1.0 / CW)
        grad_mixed = inv_std * (grad_unit - mean_unit - normed * mean_both)
        slots = grad_mixed.reshape(SIDE, SUB, CP)
        chosen_ref[pl.ds(r * GS + 8, SIDE)] = jnp.sum(jnp.where(mask, slots, 0.0), axis=1)
        low_mixed = slots.astype(bf16)
        pairs = low_mixed[:, :, :128].reshape(16, 2, SUB, 128)
        gm0_ref[pl.ds(r * GP + 3, 16), :, :128] = pairs[:, 0]
        gm0_ref[pl.ds(r * GP + 3, 16), :, 128:] = pairs[:, 1]
        gm1_ref[pl.ds(r * GW + 6, SIDE)] = low_mixed[:, :, 128:]
        return carry

    lax.fori_loop(0, QROWS, visit, 0, unroll=2)
    for c in range(3):
        cols = slice(256 * c, 256 * c + 256)
        big_ref[c * CW : (c + 1) * CW] = gup_ref[:CW, cols].astype(bf16)
        big_ref[(c + 3) * CW : (c + 4) * CW] = gdown_ref[:, cols].astype(bf16)
    rows_ref[...] = jnp.zeros_like(rows_ref)
    for t in range(3):
        total = jnp.zeros((EW, CP), f32)
        for a in range(4 + t, 7):
            x = chosen_ref[(11 + t - a) * GS : (12 + t - a) * GS]
            for b in range(7):
                total = total + x[8 - b : 8 - b + EW] * kf_ref[a * 7 + b, 0:1, :]
        rows_ref[t * EW : t * EW + EW] = total
    back_ref[...] = rows_ref[...].astype(bf16)


def taps_kernel(ext0_ref, ext1_ref, gm0_ref, gm1_ref, out_ref, acc_ref, turned_ref):
    acc_ref[...] = jnp.zeros_like(acc_ref)
    for r in range(QROWS):
        g = gm0_ref[r * GP + 3 : r * GP + 19].reshape(256, CP)
        turned_ref[:, 256 * r : 256 * r + 256] = g.T
    row = lax.broadcasted_iota(jnp.int32, (128, 128), 0)
    col = lax.broadcasted_iota(jnp.int32, (128, 128), 1)
    diagonal = row == col

    def visit(a, carry):
        turned = turned_ref[...]
        sums = [jnp.zeros((8, 128), f32) for _ in range(7)]
        for n in range(4):
            at = [ext0_ref[pl.ds((r + a) * EP + n, 16)].reshape(256, CP) for r in range(QROWS)]
            both = dot(turned, jnp.concatenate(at, axis=0))
            for out_col in range(2):
                for in_col in range(2):
                    b = 2 * n + in_col - out_col
                    if 0 <= b <= 6:
                        part = both[
                            128 * out_col : 128 * out_col + 128, 128 * in_col : 128 * in_col + 128
                        ]
                        part = jnp.where(diagonal, part, 0.0).reshape(16, 8, 128)
                        sums[b] = sums[b] + jnp.sum(part, axis=0)
        for b in range(7):
            acc_ref[a * 7 + b, :, :128] += sums[b]
        rest = [jnp.zeros((2, 8, 128), f32) for _ in range(7)]
        for r in range(QROWS):
            for block in range(4):
                x = ext1_ref[pl.ds((r + a) * EW + 8 * block, 14)].astype(f32)
                g = gm1_ref[r * GW + 6 + 8 * block : r * GW + 14 + 8 * block].astype(f32)
                x = x.reshape(14, 2, 8, 128)
                g = g.reshape(8, 2, 8, 128)
                for b in range(7):
                    for n in range(8):
                        rest[b] = rest[b] + x[b + n] * g[n]
        for b in range(7):
            acc_ref[a * 7 + b, :, 128:] += rest[b][0] + rest[b][1]
        return carry

    lax.fori_loop(0, 7, visit, 0)
    out_ref[...] = jnp.sum(acc_ref[...], axis=1)


def back_kernel(
    gm0_ref,
    gm1_ref,
    diag_ref,
    kf_ref,
    partner_ref,
    cot_ref,
    moved_ref,
    ws_ref,
    es_ref,
    links_ref,
    flags_ref,
    after_ref,
    mid_ref,
    w_ref,
    e_ref,
    gstem_ref,
    gmx0,
    gmx1,
    row,
):
    for source, target, width in ((gm0_ref, gmx0, GP), (gm1_ref, gmx1, GW)):
        edge = jnp.zeros((3 * width, SUB, target.shape[-1]), bf16)
        target[0 : 3 * width] = edge
        target[3 * width : 11 * width] = source[...]
        target[11 * width : 14 * width] = edge
        fill_halo(target, width, links_ref)

    def visit(r, carry):
        pairs = conv_pairs(gmx0, r * GP, GP, EP, diag_ref, True)
        for n in range(2):
            row[r, :, n, :, :128] = pairs[:, 128 * n : 128 * n + 128].reshape(EP, SUB, 128)
        for q in range(0, EW, 8):
            count = min(8, EW - q)
            row[r, q // 2 : (q + count) // 2, :, :, 128:] = conv_rest(
                gmx1, r * GW + q, GW, count, kf_ref, True
            ).reshape(count // 2, 2, SUB, 128)
        return carry

    lax.fori_loop(0, QROWS, visit, 0, unroll=2)
    partner = partner_ref[...]
    for k in range(3):
        for q in (0, 16, EW - 16):
            skip = 10 if q == EW - 16 else 0
            add = dot(fold_spread(flags_ref, k * EW + q), partner).reshape(16, SUB, CP)
            row[5 + k, (q + skip) // 2 : q // 2 + 8] += add[skip:].reshape(-1, 2, SUB, CP)
    for r in range(QROWS):
        full = row[r].reshape(EW, SUB, CP)
        mid_ref[r] = full[3:35]
        w_ref[3 * r : 3 * r + 3] = full[0:3].astype(bf16)
        e_ref[3 * r : 3 * r + 3] = full[35:38].astype(bf16)
    cin = moved_ref.shape[-1]
    gstem = dot_t(ws_ref[...].reshape(24 * SUB, cin), w_ref[...].reshape(24 * SUB, CP))
    gstem += dot_t(es_ref[...].reshape(24 * SUB, cin), e_ref[...].reshape(24 * SUB, CP))
    gstem_ref[...] = gstem
    for r in range(QROWS):
        own = mid_ref[r, :, :, :CW] + cot_ref[r].astype(f32)
        own = own.astype(bf16).reshape(SIDE * SUB, CW)
        gstem_ref[:, :CW] += dot_t(moved_ref[r].reshape(SIDE * SUB, cin), own)


def final_kernel(
    mid_ref, cot_ref, w_ref, e_ref, stem_t_ref, links_ref, out_ref, gout
):
    swap = swap_matrix()
    gout[...] = mid_ref[...]
    gout[:, :, :, 0:CW] = gout[:, :, :, 0:CW] + cot_ref[...].astype(f32)
    for source, column, at in ((w_ref, 0, 0), (e_ref, 1, 29)):
        matrix = side_matrix(links_ref, column)
        for start in starts(24):
            got = dot(matrix, source[start : start + 16].reshape(256, CP)).reshape(16, SUB, CP)
            for n in range(16):
                if start == 8 and n < 8:
                    continue
                r, j = divmod(start + n, 3)
                gout[r, at + j] += got[n]
    def visit(r, carry):
        for h in range(2):
            low = gout[r, 16 * h : 16 * h + 16].astype(bf16).reshape(256, CP)
            low = dot(swap, low).astype(bf16)
            grad = dot(low, stem_t_ref[...]).astype(bf16)
            for s in range(SUB):
                out_ref[s & 3, (s >> 2) * QROWS + r, 16 * h : 16 * h + 16, :] = grad[
                    16 * s : 16 * s + 16
                ]
        return carry

    lax.fori_loop(0, QROWS, visit, 0, unroll=QROWS)


def unpack_kernel(pack_ref, gstem_ref, gkernel_ref, ggain_ref, gup_ref, gdown_ref):
    count = pack_ref.shape[0] - 6 * CW
    cin = gstem_ref.shape[0]
    rest = pack_ref[:count].astype(f32)
    gstem_ref[...] = rest[:cin, :CW]
    gkernel_ref[...] = rest[cin : cin + 49, :CW]
    ggain_ref[...] = rest[cin + 49 : cin + 50, :CW]
    for c in range(3):
        cols = slice(256 * c, 256 * c + 256)
        at = count + c * CW
        gup_ref[:, cols] = pack_ref[at : at + CW].astype(f32)
        gdown_ref[cols, :] = pack_ref[at + 3 * CW : at + 4 * CW].astype(f32).T


def shifted(block, distance):
    count = lax.axis_size("tiles")
    return lax.ppermute(block, "tiles", [((i - distance) % count, i) for i in range(count)])


def levels():
    left, stride, out = lax.axis_size("tiles"), 1, []
    while left > 1:
        size = 2 if stride == 1 or left % 4 else 4
        out.append((stride, size))
        stride, left = stride * size, left // size
    return out


def rotated(block, level, distance):
    stride, size = level
    route = []
    for i in range(lax.axis_size("tiles")):
        place = (i // stride) % size
        route.append((i, i + ((place + distance) % size - place) * stride))
    return lax.ppermute(block, "tiles", route)


def place_in(level):
    stride, size = level
    return (lax.axis_index("tiles") // stride) % size


def tree_sum(terms):
    while len(terms) > 1:
        half = len(terms) // 2
        terms = [terms[n] + terms[n + half] for n in range(half)]
    return terms[0]


def scatter_sum(block, level):
    size = level[1]
    rows = block.shape[0] // size
    me = place_in(level)

    def piece(distance):
        return lax.dynamic_slice_in_dim(block, ((me + distance) % size) * rows, rows, 0)

    terms = [piece(0)] + [rotated(piece(n), level, n) for n in range(1, size)]
    return tree_sum([t.astype(f32) for t in terms]).astype(bf16)


def full_sum(block, level):
    terms = [block] + [rotated(block, level, n) for n in range(1, level[1])]
    return tree_sum([t.astype(f32) for t in terms])


def sum_kernel(*refs):
    *terms, after_ref, out_ref = refs
    rows = out_ref.shape[0]
    out_ref[...] = tree_sum([t[:rows].astype(f32) for t in terms]).astype(bf16)


def sum_and_gather(block, count, level, after):
    size = level[1]
    rows = block.shape[0] - count
    me = place_in(level)
    terms = [block] + [rotated(block, level, n) for n in range(1, size)]
    if after is None:
        total = tree_sum([t[:count].astype(f32) for t in terms]).astype(bf16)
    else:
        total = call(
            sum_kernel,
            struct((count, block.shape[1]), bf16),
            [VMEM] * size + [pl.BlockSpec(memory_space=pl.ANY)],
        )(*terms, after)
    out = jnp.zeros((rows * size,) + block.shape[1:], block.dtype)
    for n, term in enumerate(terms):
        out = lax.dynamic_update_slice_in_dim(out, term[count:], ((me - n) % size) * rows, 0)
    return jnp.concatenate([total, out], axis=0)


def body(
    ocean_state,
    cotangent,
    w_stem,
    dw_kernel,
    norm_gain,
    w_up,
    w_down,
    tile_links,
    fold_flags,
    wet_count,
):
    cin = ocean_state.shape[3]
    half_way = lax.axis_size("tiles") // 2
    pad = CP - CW
    stem_w = jnp.pad(w_stem, ((0, 0), (0, pad)))
    kb = jnp.pad(dw_kernel.reshape(49, 1, CW), ((0, 0), (0, 0), (0, pad)))
    kf = jnp.broadcast_to(kb.astype(f32), (49, 8, CP))
    diag = kb[:, :, :128] * jnp.eye(128, dtype=bf16)
    gain = jnp.pad(norm_gain, (0, pad))[None]
    up = jnp.pad(w_up, ((0, pad), (0, 0)))
    down_t = w_down.T

    strip = struct((QROWS, 3, SUB, cin), bf16)
    stem, moved, first, last = call(
        stem_kernel,
        [
            struct((QROWS, SIDE, SUB, CP), bf16),
            struct((QROWS, SIDE, SUB, cin), bf16),
            strip,
            strip,
        ],
        [VMEM, VMEM],
        micros=5,
    )(ocean_state, stem_w)
    from_west = shifted(last, 1).reshape(24, SUB, cin)
    from_east = shifted(first, -1).reshape(24, SUB, cin)
    cot = call(cot_kernel, struct((QROWS, SIDE, SUB, CW), bf16), [VMEM, SMEM], micros=5)(
        cotangent, wet_count
    )
    west_state, east_state, west, east, fold = call(
        widen_kernel,
        [struct((24, SUB, cin), bf16)] * 2
        + [struct((24, SUB, CP), bf16)] * 2
        + [struct((128, CP), bf16)],
        [VMEM] * 4 + [SMEM, SMEM],
        [pltpu.VMEM((128, CP), f32)],
    )(from_west, from_east, stem, stem_w, tile_links, fold_flags)
    partner = shifted(fold, half_way)
    ext0, ext1, gm0, gm1, big, ggain, back = call(
        front_kernel,
        [
            struct((14 * EP, SUB, CP), bf16),
            struct((14 * EW, SUB, 128), bf16),
            struct((QROWS * GP, SUB, CP), bf16),
            struct((QROWS * GW, SUB, 128), bf16),
            struct((6 * CW, CP), bf16),
            struct((8, CP), f32),
            struct((128, CP), bf16),
        ],
        [VMEM] * 11 + [SMEM, SMEM],
        [
            pltpu.VMEM((QROWS, 16, 2, SUB, CP), f32),
            pltpu.VMEM((QROWS * GS, CP), f32),
            pltpu.VMEM((128, CP), f32),
            pltpu.VMEM((CP, FF), f32),
            pltpu.VMEM((CW, FF), f32),
        ],
        micros=36,
    )(stem, west, east, partner, cot, diag, kf, gain, up, up.T, down_t, tile_links, fold_flags)
    plan = levels()
    for level in plan[:3]:
        big = scatter_sum(big, level)
    partner_back = shifted(back, half_way)
    gkernel = call(
        taps_kernel,
        struct((49, CP), f32),
        [VMEM] * 4,
        [pltpu.VMEM((49, 8, CP), f32), pltpu.VMEM((CP, QROWS * 256), bf16)],
        micros=15,
    )(ext0, ext1, gm0, gm1)
    mid, back_w, back_e, gstem = call(
        back_kernel,
        [
            struct((QROWS, SIDE, SUB, CP), f32),
            struct((24, SUB, CP), bf16),
            struct((24, SUB, CP), bf16),
            struct((cin, CP), f32),
        ],
        [VMEM] * 9 + [SMEM, SMEM, pl.BlockSpec(memory_space=pl.ANY)],
        [
            pltpu.VMEM((14 * GP, SUB, CP), bf16),
            pltpu.VMEM((14 * GW, SUB, 128), bf16),
            pltpu.VMEM((QROWS, EP, 2, SUB, CP), f32),
        ],
        micros=20,
    )(
        gm0,
        gm1,
        diag,
        kf,
        partner_back,
        cot,
        moved,
        west_state,
        east_state,
        tile_links,
        fold_flags,
        gkernel,
    )
    back_from_west = shifted(back_e, 1)
    back_from_east = shifted(back_w, -1)
    grad_state = call(
        final_kernel,
        struct(ocean_state.shape, bf16),
        [VMEM] * 5 + [SMEM],
        [pltpu.VMEM((QROWS, SIDE, SUB, CP), f32)],
        micros=8,
    )(mid, cot, back_from_west, back_from_east, stem_w.T, tile_links)
    rest = jnp.concatenate(
        [gstem, gkernel, jnp.sum(ggain, axis=0, keepdims=True), jnp.zeros((15, CP), f32)], axis=0
    )
    count = rest.shape[0]
    pack = jnp.concatenate([rest.astype(bf16), big], axis=0)
    for level in plan[:2:-1]:
        pack = full_sum(pack, level).astype(bf16)
    for level in plan[2::-1]:
        after = grad_state if level == plan[:3][-1] else None
        pack = sum_and_gather(pack, count, level, after)
    gstem, gkernel, ggain, gup, gdown = call(
        unpack_kernel,
        [
            struct((cin, CW), f32),
            struct((49, CW), f32),
            struct((1, CW), f32),
            struct((CW, FF), f32),
            struct((FF, CW), f32),
        ],
        [VMEM],
    )(pack)
    return (grad_state, gstem, gkernel.reshape(7, 7, CW), ggain[0], gup, gdown)


def solution(mesh):
    return jax.shard_map(
        body,
        mesh=mesh,
        in_specs=(
            P("tiles", None, None, None),
            P("tiles", None, None, None),
            P(),
            P(),
            P(),
            P(),
            P(),
            P("tiles", None),
            P("tiles"),
            P("tiles"),
        ),
        out_specs=(P("tiles", None, None, None), P(), P(), P(), P(), P()),
        check_vma=False,
    )
```

```python
import jax
import jax.numpy as jnp
from jax import lax
from jax.experimental import pallas as pl
from jax.experimental.pallas import tpu as pltpu
from jax.sharding import PartitionSpec as P


epsilon = 1e-06
root_half = 0.7071067811865476
inv_root_two_pi = 0.3989422804014327
SLOTS = 4
SIDE = 32
QROWS = 8
SUB = 16
CW = 192
CP = 256
FF = 768
EW = SIDE + 6
GW = SIDE + 12
EP = EW // 2
GP = GW // 2
GS = SIDE + 16
NFOLD = 3 * EW
bf16 = jnp.bfloat16
f32 = jnp.float32
VMEM = pl.BlockSpec(memory_space=pltpu.VMEM)
SMEM = pl.BlockSpec(memory_space=pltpu.SMEM)


def call(kernel, outs, specs, scratch=(), micros=1):
    single = not isinstance(outs, (list, tuple))
    return pl.pallas_call(
        kernel,
        out_shape=outs,
        in_specs=specs,
        out_specs=VMEM if single else [VMEM] * len(outs),
        scratch_shapes=list(scratch),
        compiler_params=pltpu.CompilerParams(vmem_limit_bytes=52 * 1024 * 1024),
        cost_estimate=pl.CostEstimate(
            flops=micros * 1_150_000_000, bytes_accessed=micros * 1_000_000, transcendentals=0
        ),
    )


def struct(shape, dtype):
    return jax.ShapeDtypeStruct(shape, dtype)


def dot(a, b):
    return jnp.dot(a, b, preferred_element_type=f32)


def dot_t(a, b):
    return lax.dot_general(a, b, (((0,), (0,)), ((), ())), preferred_element_type=f32)


def iotas():
    row = lax.broadcasted_iota(jnp.int32, (256, 256), 0)
    col = lax.broadcasted_iota(jnp.int32, (256, 256), 1)
    return row, col


def one_hot(mask):
    return jnp.where(mask, 1.0, 0.0).astype(bf16)


def swap_matrix():
    row, col = iotas()
    return one_hot(col == (row & 15) * 16 + (row >> 4))


def by_slot(slot, links_ref, column):
    link = jnp.full_like(slot, -1)
    for n in range(SLOTS):
        link = jnp.where(slot == n, links_ref[n, column], link)
    return link


def side_matrix(links_ref, column):
    row, col = iotas()
    s = row & 15
    link = by_slot(s & 3, links_ref, column)
    target = jnp.where(link >= 0, row - (s & 3) + link, -1)
    return one_hot(col == target)


def south_matrix(links_ref):
    row, col = iotas()
    s = row & 15
    link = by_slot(s & 3, links_ref, 2)
    target = jnp.where(s >= 4, row - 4, jnp.where(link >= 0, row - s + 12 + link, -1))
    return one_hot(col == target)


def north_matrix(links_ref):
    row, col = iotas()
    s = row & 15
    link = by_slot(s & 3, links_ref, 3)
    target = jnp.where(s < 12, row + 4, jnp.where(link >= 0, row - s + link, -1))
    return one_hot(col == target)


def starts(count):
    return [min(16 * n, count - 16) for n in range(-(-count // 16))]


def picked(matrix, block):
    lanes = block.shape[-1]
    return dot(matrix, block.reshape(256, lanes)).astype(bf16).reshape(16, SUB, lanes)


def fold_mask(flags_ref, shape):
    s = lax.broadcasted_iota(jnp.int32, shape, len(shape) - 2)
    mask = jnp.zeros(shape, jnp.int32)
    for n in range(SLOTS):
        mask = jnp.where(s == 12 + n, flags_ref[n], mask)
    return mask == 1


def fold_spread(flags_ref, start, step=1, parity=0):
    row = lax.broadcasted_iota(jnp.int32, (256, 128), 0)
    col = lax.broadcasted_iota(jnp.int32, (256, 128), 1)
    s = row & 15
    flag = jnp.zeros_like(s)
    for n in range(SLOTS):
        flag = jnp.where(s == 12 + n, flags_ref[n], flag)
    return one_hot((flag == 1) & (col == NFOLD - 1 - parity - step * (start + (row >> 4))))


def tap_of(a, b, flip):
    return (6 - a) * 7 + 6 - b if flip else a * 7 + b


def pair_weights(diag_ref, a, flip):
    def block(b):
        if 0 <= b <= 6:
            return diag_ref[tap_of(a, b, flip)]
        return jnp.zeros((128, 128), bf16)

    rows = [jnp.concatenate([block(m), block(m - 1)], axis=1) for m in range(8)]
    return jnp.concatenate(rows, axis=0)


def pair_term(src, bases, count, diag_ref, a, flip):
    parts = []
    for n in range(4):
        at = [src[pl.ds(base + n, count)].reshape(count * SUB, CP) for base in bases]
        parts.append(jnp.concatenate(at, axis=0))
    return dot(jnp.concatenate(parts, axis=1), pair_weights(diag_ref, a, flip))


def conv_pairs(src, base, width, count, diag_ref, flip):
    total = None
    for a in range(7):
        term = pair_term(src, [base + a * width], count, diag_ref, a, flip)
        total = term if total is None else total + term
    return total


def conv_rest(src, base, width, count, kf_ref, flip):
    total = jnp.zeros((count, 2, 8, 128), f32)
    for a in range(7):
        x = src[pl.ds(base + a * width, count + 6)].astype(f32).reshape(count + 6, 2, 8, 128)
        for b in range(7):
            total = total + x[b : b + count] * kf_ref[tap_of(a, b, flip), :, 128:]
    return total.reshape(count, SUB, 128)


def gelu_parts(hidden):
    cdf = 0.5 + 0.5 * lax.erf(hidden * root_half)
    bell = jnp.exp(-0.5 * hidden * hidden) * inv_root_two_pi
    return cdf, cdf + hidden * bell


def stem_kernel(state_ref, w_ref, stem_ref, moved_ref, first_ref, last_ref):
    swap = swap_matrix()
    w = w_ref[...]

    def visit(r, carry):
        for h in range(2):
            slabs = [
                state_ref[s & 3, (s >> 2) * QROWS + r, 16 * h : 16 * h + 16, :] for s in range(SUB)
            ]
            x = dot(swap, jnp.concatenate(slabs, axis=0)).astype(bf16)
            stem_ref[r, 16 * h : 16 * h + 16] = dot(x, w).astype(bf16).reshape(16, SUB, CP)
            x = x.reshape(16, SUB, -1)
            moved_ref[r, 16 * h : 16 * h + 16] = x
            if h == 0:
                first_ref[r] = x[:3]
            else:
                last_ref[r] = x[13:]
        return carry

    lax.fori_loop(0, QROWS, visit, 0, unroll=QROWS)


def cot_kernel(cot_ref, wet_ref, out_ref):
    swap = swap_matrix()

    def visit(r, carry):
        for h in range(2):
            slabs = []
            for s in range(SUB):
                slab = cot_ref[s & 3, (s >> 2) * QROWS + r, 16 * h : 16 * h + 16, :]
                slabs.append(jnp.where((s & 3) < wet_ref[0], slab, jnp.zeros_like(slab)))
            x = jnp.concatenate(slabs, axis=0)
            out_ref[r, 16 * h : 16 * h + 16] = dot(swap, x).astype(bf16).reshape(16, SUB, CW)
        return carry

    lax.fori_loop(0, QROWS, visit, 0, unroll=QROWS)


def widen_kernel(
    west_ref,
    east_ref,
    stem_ref,
    stem_w_ref,
    links_ref,
    flags_ref,
    ws_out,
    es_out,
    w_out,
    e_out,
    fold_out,
    rows,
):
    for source, column, raw, out in (
        (west_ref, 0, ws_out, w_out),
        (east_ref, 1, es_out, e_out),
    ):
        matrix = side_matrix(links_ref, column)
        for start in starts(24):
            got = picked(matrix, source[start : start + 16])
            raw[start : start + 16] = got
            got = dot(got.reshape(256, -1), stem_w_ref[...]).astype(bf16)
            out[start : start + 16] = got.reshape(16, SUB, CP)
    mask = fold_mask(flags_ref, (1, SUB, CP))
    rows[...] = jnp.zeros_like(rows)

    def chosen(block):
        return jnp.sum(jnp.where(mask, block.astype(f32), 0.0), axis=1)

    for k in range(3):
        rows[k * EW : k * EW + 3] = chosen(w_out[(5 + k) * 3 : (6 + k) * 3])
        rows[k * EW + 3 : k * EW + 35] = chosen(stem_ref[5 + k])
        rows[k * EW + 35 : k * EW + 38] = chosen(e_out[(5 + k) * 3 : (6 + k) * 3])
    fold_out[...] = rows[...].astype(bf16)


def fill_halo(ref, width, links_ref):
    south = south_matrix(links_ref)
    north = north_matrix(links_ref)
    for start in starts(3 * width):
        ref[start : start + 16] = picked(south, ref[8 * width + start : 8 * width + start + 16])
        top = 11 * width + start
        ref[top : top + 16] = picked(north, ref[3 * width + start : 3 * width + start + 16])


def front_kernel(
    stem_ref,
    w_ref,
    e_ref,
    partner_ref,
    cot_ref,
    diag_ref,
    kf_ref,
    gain_ref,
    up_ref,
    up_t_ref,
    down_t_ref,
    links_ref,
    flags_ref,
    ext0_ref,
    ext1_ref,
    gm0_ref,
    gm1_ref,
    gup_ref,
    gdown_ref,
    ggain_ref,
    back_ref,
    mixed_ref,
    chosen_ref,
    rows_ref,
):
    for r in range(QROWS):
        west, east = w_ref[3 * r : 3 * r + 3], e_ref[3 * r : 3 * r + 3]
        x = jnp.concatenate([west, stem_ref[r], east], axis=0)
        pairs = x[:, :, :128].reshape(EP, 2, SUB, 128)
        ext0_ref[(r + 3) * EP : (r + 4) * EP, :, :128] = pairs[:, 0]
        ext0_ref[(r + 3) * EP : (r + 4) * EP, :, 128:] = pairs[:, 1]
        ext1_ref[(r + 3) * EW : (r + 4) * EW] = x[:, :, 128:]
    fill_halo(ext0_ref, EP, links_ref)
    fill_halo(ext1_ref, EW, links_ref)
    partner = partner_ref[...]
    mask = fold_mask(flags_ref, (1, SUB, CP))
    for start in starts(3 * EP):
        top = 11 * EP + start
        halves = [dot(fold_spread(flags_ref, start, 2, n), partner[:, :128]) for n in range(2)]
        add = jnp.concatenate(halves, axis=1).astype(bf16).reshape(16, SUB, CP)
        ext0_ref[top : top + 16] = jnp.where(mask, add, ext0_ref[top : top + 16])
    for start in starts(NFOLD):
        top = 11 * EW + start
        add = dot(fold_spread(flags_ref, start), partner[:, 128:]).astype(bf16)
        ext1_ref[top : top + 16] = jnp.where(
            mask[:, :, :128], add.reshape(16, SUB, 128), ext1_ref[top : top + 16]
        )
    gm0_ref[...] = jnp.zeros_like(gm0_ref)
    gm1_ref[...] = jnp.zeros_like(gm1_ref)
    gup_ref[...] = jnp.zeros_like(gup_ref)
    gdown_ref[...] = jnp.zeros_like(gdown_ref)
    ggain_ref[...] = jnp.zeros_like(ggain_ref)
    chosen_ref[...] = jnp.zeros_like(chosen_ref)

    def mix(r, carry):
        pairs = conv_pairs(ext0_ref, r * EP, EP, 16, diag_ref, False)
        for n in range(2):
            half = pairs[:, 128 * n : 128 * n + 128]
            mixed_ref[r, :, n, :, :128] = half.reshape(16, SUB, 128)
        for block in range(4):
            mixed_ref[r, 4 * block : 4 * block + 4, :, :, 128:] = conv_rest(
                ext1_ref, r * EW + 8 * block, EW, 8, kf_ref, False
            ).reshape(4, 2, SUB, 128)
        return carry

    lax.fori_loop(0, QROWS, mix, 0)

    def visit(r, carry):
        mixed = mixed_ref[r].reshape(512, CP)
        lane = lax.broadcasted_iota(jnp.int32, (1, CP), 1)
        average = jnp.sum(mixed, axis=-1, keepdims=True) * (1.0 / CW)
        centred = jnp.where(lane < CW, mixed - average, 0.0)
        variance = jnp.sum(centred * centred, axis=-1, keepdims=True) * (1.0 / CW)
        inv_std = lax.rsqrt(variance + epsilon)
        normed = centred * inv_std
        gain = gain_ref[...]
        low = (normed * gain).astype(bf16)
        cot = cot_ref[r].reshape(512, CW)
        grad_normed = jnp.zeros((512, CP), f32)
        for c in range(3):
            cols = slice(256 * c, 256 * c + 256)
            hidden = dot(low, up_ref[:, cols])
            grad_act = dot(cot, down_t_ref[:, cols])
            cdf, slope = gelu_parts(hidden)
            act = (hidden * cdf).astype(bf16)
            grad_hidden = (grad_act * slope).astype(bf16)
            gdown_ref[:, cols] += dot_t(cot, act)
            gup_ref[:, cols] += dot_t(low, grad_hidden)
            grad_normed = grad_normed + dot(grad_hidden, up_t_ref[cols, :])
        product = grad_normed * normed
        ggain_ref[...] += jnp.sum(product.reshape(64, 8, CP), axis=0)
        grad_unit = grad_normed * gain
        mean_unit = jnp.sum(grad_unit, axis=-1, keepdims=True) * (1.0 / CW)
        mean_both = jnp.sum(product * gain, axis=-1, keepdims=True) * (1.0 / CW)
        grad_mixed = inv_std * (grad_unit - mean_unit - normed * mean_both)
        slots = grad_mixed.reshape(SIDE, SUB, CP)
        chosen_ref[pl.ds(r * GS + 8, SIDE)] = jnp.sum(jnp.where(mask, slots, 0.0), axis=1)
        low_mixed = slots.astype(bf16)
        pairs = low_mixed[:, :, :128].reshape(16, 2, SUB, 128)
        gm0_ref[pl.ds(r * GP + 3, 16), :, :128] = pairs[:, 0]
        gm0_ref[pl.ds(r * GP + 3, 16), :, 128:] = pairs[:, 1]
        gm1_ref[pl.ds(r * GW + 6, SIDE)] = low_mixed[:, :, 128:]
        return carry

    lax.fori_loop(0, QROWS, visit, 0, unroll=2)
    rows_ref[...] = jnp.zeros_like(rows_ref)
    for t in range(3):
        total = jnp.zeros((EW, CP), f32)
        for a in range(4 + t, 7):
            x = chosen_ref[(11 + t - a) * GS : (12 + t - a) * GS]
            for b in range(7):
                total = total + x[8 - b : 8 - b + EW] * kf_ref[a * 7 + b, 0:1, :]
        rows_ref[t * EW : t * EW + EW] = total
    back_ref[...] = rows_ref[...].astype(bf16)


def taps_kernel(ext0_ref, ext1_ref, gm0_ref, gm1_ref, out_ref, acc_ref, turned_ref):
    acc_ref[...] = jnp.zeros_like(acc_ref)
    for r in range(QROWS):
        g = gm0_ref[r * GP + 3 : r * GP + 19].reshape(256, CP)
        turned_ref[:, 256 * r : 256 * r + 256] = g.T
    row = lax.broadcasted_iota(jnp.int32, (128, 128), 0)
    col = lax.broadcasted_iota(jnp.int32, (128, 128), 1)
    diagonal = row == col

    def visit(a, carry):
        turned = turned_ref[...]
        sums = [jnp.zeros((8, 128), f32) for _ in range(7)]
        for n in range(4):
            at = [ext0_ref[pl.ds((r + a) * EP + n, 16)].reshape(256, CP) for r in range(QROWS)]
            both = dot(turned, jnp.concatenate(at, axis=0))
            for out_col in range(2):
                for in_col in range(2):
                    b = 2 * n + in_col - out_col
                    if 0 <= b <= 6:
                        part = both[
                            128 * out_col : 128 * out_col + 128, 128 * in_col : 128 * in_col + 128
                        ]
                        part = jnp.where(diagonal, part, 0.0).reshape(16, 8, 128)
                        sums[b] = sums[b] + jnp.sum(part, axis=0)
        for b in range(7):
            acc_ref[a * 7 + b, :, :128] += sums[b]
        rest = [jnp.zeros((2, 8, 128), f32) for _ in range(7)]
        for r in range(QROWS):
            for block in range(4):
                x = ext1_ref[pl.ds((r + a) * EW + 8 * block, 14)].astype(f32)
                g = gm1_ref[r * GW + 6 + 8 * block : r * GW + 14 + 8 * block].astype(f32)
                x = x.reshape(14, 2, 8, 128)
                g = g.reshape(8, 2, 8, 128)
                for b in range(7):
                    for n in range(8):
                        rest[b] = rest[b] + x[b + n] * g[n]
        for b in range(7):
            acc_ref[a * 7 + b, :, 128:] += rest[b][0] + rest[b][1]
        return carry

    lax.fori_loop(0, 7, visit, 0)
    out_ref[...] = jnp.sum(acc_ref[...], axis=1)


def back_kernel(
    gm0_ref,
    gm1_ref,
    diag_ref,
    kf_ref,
    partner_ref,
    cot_ref,
    moved_ref,
    ws_ref,
    es_ref,
    links_ref,
    flags_ref,
    after_ref,
    mid_ref,
    w_ref,
    e_ref,
    gstem_ref,
    gmx0,
    gmx1,
    row,
):
    for source, target, width in ((gm0_ref, gmx0, GP), (gm1_ref, gmx1, GW)):
        edge = jnp.zeros((3 * width, SUB, target.shape[-1]), bf16)
        target[0 : 3 * width] = edge
        target[3 * width : 11 * width] = source[...]
        target[11 * width : 14 * width] = edge
        fill_halo(target, width, links_ref)

    def visit(r, carry):
        pairs = conv_pairs(gmx0, r * GP, GP, EP, diag_ref, True)
        for n in range(2):
            row[r, :, n, :, :128] = pairs[:, 128 * n : 128 * n + 128].reshape(EP, SUB, 128)
        for q in range(0, EW, 8):
            count = min(8, EW - q)
            row[r, q // 2 : (q + count) // 2, :, :, 128:] = conv_rest(
                gmx1, r * GW + q, GW, count, kf_ref, True
            ).reshape(count // 2, 2, SUB, 128)
        return carry

    lax.fori_loop(0, QROWS, visit, 0, unroll=2)
    partner = partner_ref[...]
    for k in range(3):
        for q in (0, 16, EW - 16):
            skip = 10 if q == EW - 16 else 0
            add = dot(fold_spread(flags_ref, k * EW + q), partner).reshape(16, SUB, CP)
            row[5 + k, (q + skip) // 2 : q // 2 + 8] += add[skip:].reshape(-1, 2, SUB, CP)
    for r in range(QROWS):
        full = row[r].reshape(EW, SUB, CP)
        mid_ref[r] = full[3:35]
        w_ref[3 * r : 3 * r + 3] = full[0:3].astype(bf16)
        e_ref[3 * r : 3 * r + 3] = full[35:38].astype(bf16)
    cin = moved_ref.shape[-1]
    gstem = dot_t(ws_ref[...].reshape(24 * SUB, cin), w_ref[...].reshape(24 * SUB, CP))
    gstem += dot_t(es_ref[...].reshape(24 * SUB, cin), e_ref[...].reshape(24 * SUB, CP))
    gstem_ref[...] = gstem
    for r in range(QROWS):
        own = mid_ref[r, :, :, :CW] + cot_ref[r].astype(f32)
        own = own.astype(bf16).reshape(SIDE * SUB, CW)
        gstem_ref[:, :CW] += dot_t(moved_ref[r].reshape(SIDE * SUB, cin), own)


def final_kernel(
    mid_ref, cot_ref, w_ref, e_ref, stem_t_ref, links_ref, out_ref, gout
):
    swap = swap_matrix()
    gout[...] = mid_ref[...]
    gout[:, :, :, 0:CW] = gout[:, :, :, 0:CW] + cot_ref[...].astype(f32)
    for source, column, at in ((w_ref, 0, 0), (e_ref, 1, 29)):
        matrix = side_matrix(links_ref, column)
        for start in starts(24):
            got = dot(matrix, source[start : start + 16].reshape(256, CP)).reshape(16, SUB, CP)
            for n in range(16):
                if start == 8 and n < 8:
                    continue
                r, j = divmod(start + n, 3)
                gout[r, at + j] += got[n]
    def visit(r, carry):
        for h in range(2):
            low = gout[r, 16 * h : 16 * h + 16].astype(bf16).reshape(256, CP)
            low = dot(swap, low).astype(bf16)
            grad = dot(low, stem_t_ref[...]).astype(bf16)
            for s in range(SUB):
                out_ref[s & 3, (s >> 2) * QROWS + r, 16 * h : 16 * h + 16, :] = grad[
                    16 * s : 16 * s + 16
                ]
        return carry

    lax.fori_loop(0, QROWS, visit, 0, unroll=QROWS)


def shifted(block, distance):
    count = lax.axis_size("tiles")
    return lax.ppermute(block, "tiles", [((i - distance) % count, i) for i in range(count)])


def levels():
    left, stride, out = lax.axis_size("tiles"), 1, []
    while left > 1:
        size = 2 if stride == 1 or left % 4 else 4
        out.append((stride, size))
        stride, left = stride * size, left // size
    return out


def rotated(block, level, distance):
    stride, size = level
    route = []
    for i in range(lax.axis_size("tiles")):
        place = (i // stride) % size
        route.append((i, i + ((place + distance) % size - place) * stride))
    return lax.ppermute(block, "tiles", route)


def place_in(level):
    stride, size = level
    return (lax.axis_index("tiles") // stride) % size


def tree_sum(terms):
    while len(terms) > 1:
        half = len(terms) // 2
        terms = [terms[n] + terms[n + half] for n in range(half)]
    return terms[0]


def scatter_sum(block, level):
    size = level[1]
    rows = block.shape[0] // size
    me = place_in(level)

    def piece(distance):
        return lax.dynamic_slice_in_dim(block, ((me + distance) % size) * rows, rows, 0)

    terms = [piece(0)] + [rotated(piece(n), level, n) for n in range(1, size)]
    return tree_sum([t.astype(f32) for t in terms]).astype(bf16)


def full_sum(block, level, after=None):
    terms = [block] + [rotated(block, level, n) for n in range(1, level[1])]
    return summed(terms, block.shape[0], after)


def sum_kernel(*refs):
    *terms, after_ref, out_ref = refs
    rows = out_ref.shape[0]
    out_ref[...] = tree_sum([t[:rows].astype(f32) for t in terms]).astype(bf16)


def summed(terms, count, after):
    if after is None:
        return tree_sum([t[:count].astype(f32) for t in terms]).astype(bf16)
    return call(
        sum_kernel,
        struct((count, terms[0].shape[1]), bf16),
        [VMEM] * len(terms) + [pl.BlockSpec(memory_space=pl.ANY)],
    )(*terms, after)


def sum_and_gather(block, count, level, after):
    size = level[1]
    rows = block.shape[0] - count
    me = place_in(level)
    terms = [block] + [rotated(block, level, n) for n in range(1, size)]
    total = summed(terms, count, after)
    out = jnp.zeros((rows * size,) + block.shape[1:], block.dtype)
    for n, term in enumerate(terms):
        out = lax.dynamic_update_slice_in_dim(out, term[count:], ((me - n) % size) * rows, 0)
    return jnp.concatenate([total, out], axis=0)


def body(
    ocean_state,
    cotangent,
    w_stem,
    dw_kernel,
    norm_gain,
    w_up,
    w_down,
    tile_links,
    fold_flags,
    wet_count,
):
    cin = ocean_state.shape[3]
    half_way = lax.axis_size("tiles") // 2
    pad = CP - CW
    stem_w = jnp.pad(w_stem, ((0, 0), (0, pad)))
    kb = jnp.pad(dw_kernel.reshape(49, 1, CW), ((0, 0), (0, 0), (0, pad)))
    kf = jnp.broadcast_to(kb.astype(f32), (49, 8, CP))
    diag = kb[:, :, :128] * jnp.eye(128, dtype=bf16)
    gain = jnp.pad(norm_gain, (0, pad))[None]
    up = jnp.pad(w_up, ((0, pad), (0, 0)))
    down_t = w_down.T

    strip = struct((QROWS, 3, SUB, cin), bf16)
    stem, moved, first, last = call(
        stem_kernel,
        [
            struct((QROWS, SIDE, SUB, CP), bf16),
            struct((QROWS, SIDE, SUB, cin), bf16),
            strip,
            strip,
        ],
        [VMEM, VMEM],
        micros=5,
    )(ocean_state, stem_w)
    from_west = shifted(last, 1).reshape(24, SUB, cin)
    from_east = shifted(first, -1).reshape(24, SUB, cin)
    cot = call(cot_kernel, struct((QROWS, SIDE, SUB, CW), bf16), [VMEM, SMEM], micros=5)(
        cotangent, wet_count
    )
    west_state, east_state, west, east, fold = call(
        widen_kernel,
        [struct((24, SUB, cin), bf16)] * 2
        + [struct((24, SUB, CP), bf16)] * 2
        + [struct((128, CP), bf16)],
        [VMEM] * 4 + [SMEM, SMEM],
        [pltpu.VMEM((128, CP), f32)],
    )(from_west, from_east, stem, stem_w, tile_links, fold_flags)
    partner = shifted(fold, half_way)
    ext0, ext1, gm0, gm1, gup, gdown, ggain, back = call(
        front_kernel,
        [
            struct((14 * EP, SUB, CP), bf16),
            struct((14 * EW, SUB, 128), bf16),
            struct((QROWS * GP, SUB, CP), bf16),
            struct((QROWS * GW, SUB, 128), bf16),
            struct((CP, FF), f32),
            struct((CW, FF), f32),
            struct((8, CP), f32),
            struct((128, CP), bf16),
        ],
        [VMEM] * 11 + [SMEM, SMEM],
        [
            pltpu.VMEM((QROWS, 16, 2, SUB, CP), f32),
            pltpu.VMEM((QROWS * GS, CP), f32),
            pltpu.VMEM((128, CP), f32),
        ],
        micros=36,
    )(stem, west, east, partner, cot, diag, kf, gain, up, up.T, down_t, tile_links, fold_flags)
    parts = [g[:CW, 256 * c : 256 * c + 256] for g in (gup, gdown) for c in range(3)]
    big = jnp.concatenate(parts, axis=0).astype(bf16)
    plan = levels()
    for level in plan[:3]:
        big = scatter_sum(big, level)
    partner_back = shifted(back, half_way)
    gkernel = call(
        taps_kernel,
        struct((49, CP), f32),
        [VMEM] * 4,
        [pltpu.VMEM((49, 8, CP), f32), pltpu.VMEM((CP, QROWS * 256), bf16)],
        micros=15,
    )(ext0, ext1, gm0, gm1)
    mid, back_w, back_e, gstem = call(
        back_kernel,
        [
            struct((QROWS, SIDE, SUB, CP), f32),
            struct((24, SUB, CP), bf16),
            struct((24, SUB, CP), bf16),
            struct((cin, CP), f32),
        ],
        [VMEM] * 9 + [SMEM, SMEM, pl.BlockSpec(memory_space=pl.ANY)],
        [
            pltpu.VMEM((14 * GP, SUB, CP), bf16),
            pltpu.VMEM((14 * GW, SUB, 128), bf16),
            pltpu.VMEM((QROWS, EP, 2, SUB, CP), f32),
        ],
        micros=20,
    )(
        gm0,
        gm1,
        diag,
        kf,
        partner_back,
        cot,
        moved,
        west_state,
        east_state,
        tile_links,
        fold_flags,
        gkernel,
    )
    back_from_west = shifted(back_e, 1)
    back_from_east = shifted(back_w, -1)
    grad_state = call(
        final_kernel,
        struct(ocean_state.shape, bf16),
        [VMEM] * 5 + [SMEM],
        [pltpu.VMEM((QROWS, SIDE, SUB, CP), f32)],
        micros=8,
    )(mid, cot, back_from_west, back_from_east, stem_w.T, tile_links)
    rest = jnp.concatenate(
        [gstem, gkernel, jnp.sum(ggain, axis=0, keepdims=True), jnp.zeros((15, CP), f32)], axis=0
    )
    count = rest.shape[0]
    pack = jnp.concatenate([rest.astype(bf16), big], axis=0)
    order = plan[:2:-1] + plan[2::-1]
    for level in order:
        after = grad_state if level == order[0] else None
        if level in plan[:3]:
            pack = sum_and_gather(pack, count, level, after)
        else:
            pack = full_sum(pack, level, after)
    rest = pack[:count].astype(f32)
    big = pack[count:].astype(f32).reshape(2, 3, CW, CP)
    gup = jnp.concatenate([big[0, c] for c in range(3)], axis=1)
    gdown = jnp.concatenate([big[1, c].T for c in range(3)], axis=0)
    gstem, gkernel, ggain = rest[:cin, :CW], rest[cin : cin + 49, :CW], rest[cin + 49, :CW]
    return (grad_state, gstem, gkernel.reshape(7, 7, CW), ggain, gup, gdown)


def solution(mesh):
    return jax.shard_map(
        body,
        mesh=mesh,
        in_specs=(
            P("tiles", None, None, None),
            P("tiles", None, None, None),
            P(),
            P(),
            P(),
            P(),
            P(),
            P("tiles", None),
            P("tiles"),
            P("tiles"),
        ),
        out_specs=(P("tiles", None, None, None), P(), P(), P(), P(), P()),
        check_vma=False,
    )
```
